256 devices in a mesh: tracer: 16 (over z_lo, x, core), space: 16 (over z_hi, y).
Axes of the slice: x: 4, y: 4, z: 8 (z_hi: 4, z_lo: 2; z = z_hi * 2 + z_lo), core: 2. Of those that a mesh axis runs over, the one named last changes fastest.
Arguments:
- tracers: float32 [512, 16, 288, 128], P('tracer', None, 'space'), may hold values from -6 to 6
- met_codes: bfloat16 [16, 3, 288, 128], P('tracer', None, 'space'), may hold values from -1 to 1
- met_scales: bfloat16 [16, 3, 288], P('tracer', None, 'space'), may hold values from 0.29882812 to 0.8984375
- owner_slot: int32 [16], replicated, may hold values from 0 to 15, each once
- conv_weight: float32 [288, 128], P('space'), may hold values from 0.2 to 0.9
- cloud_top: int32 [288, 128], P('space'), may hold values from 1 to 16
- emission: float32 [288, 128], P('space'), may hold values from 0.5 to 2
- region_tag: int32 [288, 128], P('space'), may hold values from 0 to 511
Outputs:
- tracers_out: float32 [512, 16, 288, 128], P('tracer', None, 'space')
The draws below stay inside these ranges and needn't reach their ends.
Inputs may be any that keep to these rules, and one draw needn't show every extreme that they name: owner_slot names every slot 0 to 15 once.
All inputs are finite; a program needn't handle non-finite values.
Results may differ from the reference program's by a relative error of at most 0.0003.
Values may be sent and summed in bfloat16 or wider, within the bound.
A program may use at most 128 MiB of HBM per device.

```python
import math
import jax
import jax.numpy as jnp
from jax import lax

TR_DEV = 32
LEV = 16
LAT = 128
SUBSTEPS = 2
TRACERS = 512
NLON = 288
PIECES = 16
PROWS = 3


def place_ends(entries, stream_key, low, top_value):
    dims = entries.shape
    place = [jax.random.randint(jax.random.fold_in(stream_key, axis), (), 0, dims[axis]) for axis in range(len(dims))]
    entries = entries.at[tuple(place)].set(low)
    longest = dims.index(max(dims))
    place[longest] = (place[longest] + 1) % dims[longest]
    return entries.at[tuple(place)].set(top_value)


def block_levels(own_key, shape, cuts, least, largest):
    gain = 1.0
    for axis_at, parts in cuts:
        draws = jax.random.uniform(jax.random.fold_in(jax.random.fold_in(own_key, 6), axis_at), (parts,), jnp.float32, least / len(cuts), largest / len(cuts))
        gain = gain * jnp.repeat(jnp.exp(draws), shape[axis_at] // parts).reshape((-1,) + (1,) * (len(shape) - 1 - axis_at))
    return gain


def noise(rng, extent, width, limit, pieces=(), kind=jnp.bfloat16):
    level = block_levels(rng, extent, pieces, -0.22, 0.18) if pieces else 1.0
    drawn = jax.random.normal(rng, extent, jnp.float32) * width * level
    return jnp.minimum(jnp.maximum(drawn, -limit), limit).astype(kind)


def setup_inputs(seed: int = 0) -> dict:
    key_list = jax.random.split(jax.random.key(seed), 9)
    tracers = noise(key_list[0], (TRACERS, LEV, NLON, LAT), 1.0, 6.0, ((0, 16), (2, 16)), jnp.float32)
    met_codes = jnp.clip(jax.random.uniform(key_list[1], (PIECES, PROWS, NLON, LAT), jnp.float32, -1.0, 1.0) * block_levels(key_list[1], (PIECES, PROWS, NLON, LAT), ((0, 16), (2, 16)), -0.4, 0.0), -1.0, 1.0).astype(jnp.bfloat16)
    met_scales = jnp.clip(jnp.exp(math.log(0.8984375) - 1.1007886 * jax.random.uniform(key_list[2], (PIECES, PROWS, NLON), jnp.float32) ** block_levels(key_list[2], (PIECES, PROWS, NLON), ((0, 16), (2, 16)), -0.2, 0.2)), 0.29882812, 0.8984375).astype(jnp.bfloat16)
    owner_slot = jax.random.permutation(key_list[3], PIECES).astype(jnp.int32)
    conv_weight = jnp.clip(0.2 + 0.7 * jax.random.uniform(key_list[4], (NLON, LAT), jnp.float32) ** block_levels(key_list[4], (NLON, LAT), ((0, 16),), -0.2, 0.2), 0.2, 0.9)
    cloud_top = place_ends(jax.random.randint(key_list[5], (NLON, LAT), 1, LEV + 1), jax.random.fold_in(key_list[5], 1), 1, LEV).astype(jnp.int32)
    emission = jnp.clip(jnp.exp(math.log(2.0) - 1.3862944 * jax.random.uniform(key_list[6], (NLON, LAT), jnp.float32) ** block_levels(key_list[6], (NLON, LAT), ((0, 16),), -0.2, 0.2)), 0.5, 2.0)
    region_tag = place_ends(jax.random.randint(key_list[7], (NLON, LAT), 0, TRACERS), jax.random.fold_in(key_list[7], 1), 0, TRACERS - 1).astype(jnp.int32)
    return {"tracers": tracers, "met_codes": met_codes, "met_scales": met_scales, "owner_slot": owner_slot, "conv_weight": conv_weight, "cloud_top": cloud_top, "emission": emission, "region_tag": region_tag}


def fromm_flux(courant, left_val, left_slope, right_val, right_slope):
    upwind_left = courant * (left_val + 0.5 * (1.0 - courant) * left_slope)
    upwind_right = courant * (right_val - 0.5 * (1.0 + courant) * right_slope)
    return jnp.where(courant > 0, upwind_left, upwind_right)


def sweep_east(extended, face_courant):
    cells = extended.shape[-2] - 4
    slope = 0.5 * (extended[..., 2:, :] - extended[..., :-2, :])
    flux = fromm_flux(face_courant, extended[..., 1:cells + 2, :], slope[..., 0:cells + 1, :],
                      extended[..., 2:cells + 3, :], slope[..., 1:cells + 2, :])
    return extended[..., 2:cells + 2, :] - (flux[..., 1:, :] - flux[..., :-1, :])


def sweep_north(mixing, courant_south):
    rows = mixing.shape[-1]
    widths = [(0, 0)] * (mixing.ndim - 1) + [(2, 2)]
    padded = jnp.pad(mixing, widths)
    slope = 0.5 * (padded[..., 2:] - padded[..., :-2])
    walled = courant_south * (jnp.arange(rows) > 0).astype(jnp.float32)
    flux = fromm_flux(walled, padded[..., 1:rows + 1], slope[..., 0:rows],
                      padded[..., 2:rows + 2], slope[..., 1:rows + 1])
    upper = jnp.concatenate([flux[..., 1:], jnp.zeros_like(flux[..., :1])], axis=-1)
    return mixing - (upper - flux)


def convect(mixing, air_mass, strength, top_level):
    levels = air_mass.shape[0]
    in_cloud = (jnp.arange(levels, dtype=jnp.int32)[:, None, None] < top_level[None]).astype(jnp.float32)
    weighted = in_cloud * air_mass
    cloud_mass = jnp.sum(weighted, axis=0)
    cloud_mean = jnp.sum(weighted * mixing, axis=-3) / cloud_mass
    return mixing + strength * in_cloud * (cloud_mean[:, None] - mixing)


def later_sweeps(mixing, column_met, levels):
    mixing = sweep_north(mixing, column_met[levels:2 * levels])
    air_mass = 1.0 + 0.5 * column_met[2 * levels:3 * levels]
    top_level = column_met[3 * levels + 1].astype(jnp.int32)
    return convect(mixing, air_mass, column_met[3 * levels], top_level)


def reference(tracers, met_codes, met_scales, owner_slot, conv_weight, cloud_top, emission, region_tag):
    ordered = met_codes[owner_slot].astype(jnp.float32) * met_scales[owner_slot].astype(jnp.float32)[..., None]
    met_stack = ordered.reshape(3 * LEV, NLON, LAT)
    column_met = jnp.concatenate([met_stack, conv_weight[None], cloud_top[None].astype(jnp.float32)], axis=0)
    east_courant = jnp.concatenate([met_stack[:LEV, -1:], met_stack[:LEV]], axis=1)
    blocks = tracers.reshape(TRACERS // TR_DEV, TR_DEV, LEV, NLON, LAT)
    firsts = jnp.arange(TRACERS // TR_DEV, dtype=jnp.int32) * TR_DEV

    def one_block(inputs):
        mixing, first_tracer = inputs
        tracer_ids = first_tracer + jnp.arange(TR_DEV, dtype=jnp.int32)
        emitted = (region_tag[None] == tracer_ids[:, None, None]).astype(jnp.float32) * emission[None]
        mixing = mixing.at[:, 0].add(emitted)
        for substep in range(SUBSTEPS):
            extended = jnp.concatenate([mixing[..., -2:, :], mixing, mixing[..., :2, :]], axis=-2)
            mixing = sweep_east(extended, east_courant)
            mixing = later_sweeps(mixing, column_met, LEV)
        return mixing

    result = lax.map(one_block, (blocks, firsts))
    return result.reshape(TRACERS, LEV, NLON, LAT)
```

```python
import functools

import jax
import jax.numpy as jnp
from jax import lax
from jax.experimental import pallas as pl
from jax.experimental.pallas import tpu as pltpu
from jax.sharding import PartitionSpec as P

MESH = pl.DeviceIdType.MESH
EAST, WEST = 0, 1
HIGH, LOW = 0, 1
UNROLL = 4
BLOCKS = 4
FIELDS = 12
ROW_PITCH = 24
PIECE_ROWS = 80


def face_parts(c):
    size = jnp.abs(c)
    bend = 0.25 * size * (1.0 - size)
    up = c > 0
    zero = jnp.zeros_like(c)
    return (
        jnp.where(up, -bend, zero),
        jnp.where(up, c, -bend),
        jnp.where(up, bend, c),
        jnp.where(up, zero, bend),
    )


def column_step(cells, parts):
    ea, eb, ec, ed, ee, na, nb, nc, nd, ne, share, cloud = parts
    x = ea * cells[0] + eb * cells[1] + ec * cells[2] + ed * cells[3] + ee * cells[4]
    lanes = x.ndim - 1
    size = x.shape[-1]
    y = (
        nc * x
        + na * pltpu.roll(x, 2, lanes)
        + nb * pltpu.roll(x, 1, lanes)
        + nd * pltpu.roll(x, size - 1, lanes)
        + ne * pltpu.roll(x, size - 2, lanes)
    )
    mean = jnp.sum(share * y, axis=-2, keepdims=True)
    return y + cloud * mean


def step_kernel(
    tracer_devices,
    space_devices,
    x_hbm,
    codes_ref,
    scales_ref,
    slot_ref,
    strength_ref,
    top_ref,
    emission_ref,
    tag_ref,
    out_hbm,
    q0,
    q1,
    pieces,
    staged,
    rows,
    met,
    coef,
    west_c,
    east_c,
    halo_out,
    halo_in,
    load_sem,
    store_sem,
    piece_send,
    piece_recv,
    west_send,
    west_recv,
    halo_send,
    halo_recv,
):
    count, lons, levels, lats = x_hbm.shape
    last = lons - 1
    t_me = lax.axis_index("tracer")
    s_me = lax.axis_index("space")
    east = {"space": lax.rem(s_me + 1, space_devices)}
    west = {"space": lax.rem(s_me + space_devices - 1, space_devices)}
    toward = (east, west)
    block = count // BLOCKS

    loads = [
        pltpu.make_async_copy(x_hbm.at[:, lo:hi], q0.at[:, lo:hi], load_sem.at[n])
        for n, (lo, hi) in enumerate(((0, 2), (lons - 2, lons), (2, lons - 2)))
    ]
    for copy in loads:
        copy.start()

    barrier = pltpu.get_barrier_semaphore()
    for k in range(1, tracer_devices):
        pl.semaphore_signal(
            barrier,
            inc=1,
            device_id={"tracer": lax.rem(t_me + k, tracer_devices)},
            device_id_type=MESH,
        )
    for to in toward:
        pl.semaphore_signal(barrier, inc=1, device_id=to, device_id_type=MESH)

    staged[...] = jnp.zeros_like(staged)
    for r in range(codes_ref.shape[1]):
        staged[r * ROW_PITCH : r * ROW_PITCH + lons, :] = codes_ref[0, r].astype(jnp.float32)
        staged[r * ROW_PITCH + lons : r * ROW_PITCH + lons + 1, 0:lons] = scales_ref[
            0, r : r + 1, :
        ].astype(jnp.float32)
    pieces[t_me] = staged[...].astype(jnp.bfloat16)

    pl.semaphore_wait(barrier, tracer_devices - 1 + 2)

    piece_copies = []
    for k in range(1, tracer_devices):
        copy = pltpu.make_async_remote_copy(
            src_ref=pieces.at[t_me],
            dst_ref=pieces.at[t_me],
            send_sem=piece_send.at[k],
            recv_sem=piece_recv.at[k],
            device_id={"tracer": lax.rem(t_me + k, tracer_devices)},
            device_id_type=MESH,
        )
        copy.start()
        piece_copies.append(copy)

    first = t_me * count
    level_row = lax.broadcasted_iota(jnp.int32, (8, lats), 0)

    def emit(lon):
        tag = jnp.where(level_row == 0, tag_ref[pl.ds(lon, 1), :], -1)
        amount = jnp.broadcast_to(emission_ref[pl.ds(lon, 1), :], (8, lats))

        def some(n, _):
            for u in range(UNROLL):
                t = n * UNROLL + u
                old = q0[t, lon, 0:8, :]
                q0[t, lon, 0:8, :] = old + jnp.where(tag == first + t, amount, 0.0)
            return 0

        lax.fori_loop(0, count // UNROLL, some, 0)

    loads[0].wait()
    loads[1].wait()
    for lon in (0, 1, last - 1, last):
        emit(lon)

    def halo_copy(substep, way, part, blk):
        picked = (substep, way, part, pl.ds(blk * block, block))
        return pltpu.make_async_remote_copy(
            src_ref=halo_out.at[picked],
            dst_ref=halo_in.at[picked],
            send_sem=halo_send.at[substep, way, part, blk],
            recv_sem=halo_recv.at[substep, way, part, blk],
            device_id=toward[way],
            device_id_type=MESH,
        )

    def each_block(act):
        def one(blk, _):
            act(blk)
            return 0

        lax.fori_loop(0, BLOCKS, one, 0)

    def stage_high(q, substep, way, blk):
        lon = last if way == EAST else 0

        def some(n, _):
            t = blk * block + n * UNROLL
            halo_out[substep, way, HIGH, pl.ds(t, UNROLL)] = q[pl.ds(t, UNROLL), lon].astype(
                jnp.bfloat16
            )
            return 0

        lax.fori_loop(0, block // UNROLL, some, 0)

    def stage_low(q, substep, way, blk):
        near, far = (last, last - 1) if way == EAST else (0, 1)
        if way == EAST:
            bend = 0.25 * (1.0 - east_c[...])
        else:
            bend = 0.25 * (1.0 + west_c[...])

        def some(n, _):
            t = pl.ds(blk * block + n * UNROLL, UNROLL)
            high = halo_out[substep, way, HIGH, t].astype(jnp.float32)
            rest = (q[t, near] - high) - bend * q[t, far]
            halo_out[substep, way, LOW, t] = rest.astype(jnp.bfloat16)
            return 0

        lax.fori_loop(0, block // UNROLL, some, 0)

    def first_highs(blk):
        for way in (EAST, WEST):
            stage_high(q0, 0, way, blk)
            halo_copy(0, way, HIGH, blk).start()

    each_block(first_highs)

    loads[2].wait()

    def emit_inside(n, _):
        emit(n + 2)
        return 0

    lax.fori_loop(0, lons - 4, emit_inside, 0)

    for copy in piece_copies:
        copy.wait_recv()

    piece_count = slot_ref.shape[0]
    for j in range(piece_count):
        held = pieces[slot_ref[j]].astype(jnp.float32)
        rows[j * 3 * ROW_PITCH : (j + 1) * 3 * ROW_PITCH, :] = held[: 3 * ROW_PITCH]
    stack = 3 * piece_count
    scales = rows[pl.ds(lons, stack, stride=ROW_PITCH), :]
    for lon in range(lons):
        code = rows[pl.ds(lon, stack, stride=ROW_PITCH), :]
        met[lon] = code * scales[:, lon : lon + 1]

    east_c[...] = met[last, 0:levels, :]
    west_copy = pltpu.make_async_remote_copy(
        src_ref=east_c,
        dst_ref=west_c,
        send_sem=west_send,
        recv_sem=west_recv,
        device_id=east,
        device_id_type=MESH,
    )
    west_copy.start()

    def first_lows(way):
        def act(blk):
            stage_low(q0, 0, way, blk)
            halo_copy(0, way, LOW, blk).start()

        each_block(act)

    first_lows(EAST)

    lane = lax.broadcasted_iota(jnp.int32, (levels, lats), 1)
    level = lax.broadcasted_iota(jnp.int32, (levels, lats), 0)

    def east_parts(lon, before, here):
        la, lb, lc, ld = face_parts(before)
        ra, rb, rc, rd = face_parts(here)
        coef[lon, 0] = la
        coef[lon, 1] = lb - ra
        coef[lon, 2] = 1.0 + lc - rb
        coef[lon, 3] = ld - rc
        coef[lon, 4] = -rd

    def other_parts(lon):
        south = jnp.where(lane > 0, met[lon, levels : 2 * levels, :], 0.0)
        sa, sb, sc, sd = face_parts(south)
        ua, ub, uc, ud = (pltpu.roll(p, lats - 1, 1) for p in (sa, sb, sc, sd))
        air = 1.0 + 0.5 * met[lon, 2 * levels : 3 * levels, :]
        cloud = (level < top_ref[pl.ds(lon, 1), :]).astype(jnp.float32)
        strength = strength_ref[pl.ds(lon, 1), :]
        weighted = cloud * air
        mass = jnp.sum(weighted, axis=0, keepdims=True)
        keep = 1.0 - strength * cloud
        coef[lon, 5] = keep * jnp.where(lane > 1, sa, 0.0)
        coef[lon, 6] = keep * jnp.where(lane > 0, sb - ua, 0.0)
        coef[lon, 7] = keep * (1.0 + sc - ub)
        coef[lon, 8] = keep * jnp.where(lane < lats - 1, sd - uc, 0.0)
        coef[lon, 9] = keep * jnp.where(lane < lats - 2, -ud, 0.0)
        coef[lon, 10] = strength * weighted / (mass * keep)
        coef[lon, 11] = cloud

    def all_parts(lon, _):
        east_parts(lon, met[lon - 1, 0:levels, :], met[lon, 0:levels, :])
        other_parts(lon)
        return 0

    lax.fori_loop(1, lons, all_parts, 0)
    other_parts(0)
    coef[last, 4] = -jnp.minimum(east_c[...], 0.0)

    def inside(source, target, start, stop):
        def one(lon, _):
            parts = tuple(coef[lon, f] for f in range(FIELDS))

            def some(n, _):
                t = pl.ds(n * UNROLL, UNROLL)
                cells = [source[t, lon + d] for d in (-2, -1, 0, 1, 2)]
                target[t, lon] = column_step(cells, parts)
                return 0

            lax.fori_loop(0, count // UNROLL, some, 0)
            return 0

        lax.fori_loop(start, stop, one, 0)

    def edges(source, target, substep, blk):
        for lon in (0, 1, last - 1, last):
            parts = tuple(coef[lon, f] for f in range(FIELDS))

            def some(n, _):
                t = pl.ds(blk * block + n * UNROLL, UNROLL)

                def cell(place):
                    if 0 <= place <= last:
                        return source[t, place]
                    way = EAST if place < 0 else WEST
                    part = HIGH if place in (-1, last + 1) else LOW
                    return halo_in[substep, way, part, t].astype(jnp.float32)

                cells = [cell(lon + d) for d in (-2, -1, 0, 1, 2)]
                target[t, lon] = column_step(cells, parts)
                return 0

            lax.fori_loop(0, block // UNROLL, some, 0)

    middle = 2 + (lons - 4) // 2
    inside(q0, q1, 2, middle)
    west_copy.wait()
    first_lows(WEST)
    east_parts(0, west_c[...], met[0, 0:levels, :])
    coef[0, 0] = jnp.maximum(west_c[...], 0.0)
    inside(q0, q1, middle, lons - 2)

    def first_edges(blk):
        for way in (EAST, WEST):
            for part in (HIGH, LOW):
                halo_copy(0, way, part, blk).wait_recv()
        edges(q0, q1, 0, blk)
        for way in (EAST, WEST):
            stage_high(q1, 1, way, blk)
            stage_low(q1, 1, way, blk)
            for part in (HIGH, LOW):
                halo_copy(1, way, part, blk).start()

    each_block(first_edges)

    inside(q1, q0, 2, lons - 2)
    inner = pltpu.make_async_copy(
        q0.at[:, 2 : lons - 2], out_hbm.at[:, 2 : lons - 2], store_sem.at[0]
    )
    inner.start()

    def second_edges(blk):
        for way in (EAST, WEST):
            for part in (HIGH, LOW):
                halo_copy(1, way, part, blk).wait_recv()
        edges(q1, q0, 1, blk)

    each_block(second_edges)
    outer = [
        pltpu.make_async_copy(q0.at[:, lo:hi], out_hbm.at[:, lo:hi], store_sem.at[n])
        for n, (lo, hi) in ((1, (0, 2)), (2, (lons - 2, lons)))
    ]
    for copy in outer:
        copy.start()

    def drain(blk):
        for substep in (0, 1):
            for way in (EAST, WEST):
                for part in (HIGH, LOW):
                    halo_copy(substep, way, part, blk).wait_send()

    each_block(drain)
    for copy in piece_copies:
        copy.wait_send()
    inner.wait()
    for copy in outer:
        copy.wait()


def local(tracer_devices, space_devices, tracers, met_codes, met_scales, owner_slot, conv_weight,
          cloud_top, emission, region_tag):
    by_lon = jnp.transpose(tracers, (0, 2, 1, 3))
    count, lons, levels, lats = by_lon.shape
    pieces = owner_slot.shape[0]
    stack = pieces * met_codes.shape[1]
    halo = (2, 2, 2, count, levels, lats)
    vmem = pl.BlockSpec(memory_space=pltpu.VMEM)
    hbm = pl.BlockSpec(memory_space=pl.ANY)
    out = pl.pallas_call(
        functools.partial(step_kernel, tracer_devices, space_devices),
        out_shape=jax.ShapeDtypeStruct(by_lon.shape, jnp.float32),
        in_specs=[hbm, vmem, vmem, pl.BlockSpec(memory_space=pltpu.SMEM)] + [vmem] * 4,
        out_specs=hbm,
        scratch_shapes=[
            pltpu.VMEM(by_lon.shape, jnp.float32),
            pltpu.VMEM(by_lon.shape, jnp.float32),
            pltpu.VMEM((pieces, PIECE_ROWS, lats), jnp.bfloat16),
            pltpu.VMEM((PIECE_ROWS, lats), jnp.float32),
            pltpu.VMEM((pieces * 3 * ROW_PITCH, lats), jnp.float32),
            pltpu.VMEM((lons, stack, lats), jnp.float32),
            pltpu.VMEM((lons, FIELDS, levels, lats), jnp.float32),
            pltpu.VMEM((levels, lats), jnp.float32),
            pltpu.VMEM((levels, lats), jnp.float32),
            pltpu.VMEM(halo, jnp.bfloat16),
            pltpu.VMEM(halo, jnp.bfloat16),
            pltpu.SemaphoreType.DMA((3,)),
            pltpu.SemaphoreType.DMA((3,)),
            pltpu.SemaphoreType.DMA((pieces,)),
            pltpu.SemaphoreType.DMA((pieces,)),
            pltpu.SemaphoreType.DMA,
            pltpu.SemaphoreType.DMA,
            pltpu.SemaphoreType.DMA((2, 2, 2, BLOCKS)),
            pltpu.SemaphoreType.DMA((2, 2, 2, BLOCKS)),
        ],
        compiler_params=pltpu.CompilerParams(
            collective_id=0, has_side_effects=True, vmem_limit_bytes=48 * 1024 * 1024
        ),
        name="transport_step",
    )(by_lon, met_codes, met_scales, owner_slot, conv_weight, cloud_top, emission, region_tag)
    return jnp.transpose(out, (0, 2, 1, 3))


def solution(mesh):
    placed = (
        P("tracer", None, "space", None),
        P("tracer", None, "space", None),
        P("tracer", None, "space"),
        P(),
        P("space", None),
        P("space", None),
        P("space", None),
        P("space", None),
    )
    return jax.shard_map(
        functools.partial(local, mesh.shape["tracer"], mesh.shape["space"]),
        mesh=mesh,
        in_specs=placed,
        out_specs=P("tracer", None, "space", None),
        check_vma=False,
    )
```

```python
import functools

import jax
import jax.numpy as jnp
from jax import lax
from jax.experimental import pallas as pl
from jax.experimental.pallas import tpu as pltpu
from jax.sharding import PartitionSpec as P

MESH = pl.DeviceIdType.MESH
EAST, WEST = 0, 1
HIGH, LOW = 0, 1
BLOCKS = 4
FIELDS = 12
ROW_PITCH = 24
PIECE_ROWS = 80
CORES = 2
PAIR = 2


def face_parts(c):
    size = jnp.abs(c)
    bend = 0.25 * size * (1.0 - size)
    up = c > 0
    zero = jnp.zeros_like(c)
    return (
        jnp.where(up, -bend, zero),
        jnp.where(up, c, -bend),
        jnp.where(up, bend, c),
        jnp.where(up, zero, bend),
    )


def column_step(cells, parts, shift):
    ea, eb, ec, ed, ee, na, nb, nc, nd, ne, share, cloud = parts
    x = ea * cells[0] + eb * cells[1] + ec * cells[2] + ed * cells[3] + ee * cells[4]
    count, levels, lats = x.shape
    high = x.astype(jnp.bfloat16)
    low = (x - high.astype(jnp.float32)).astype(jnp.bfloat16)
    both = jnp.concatenate([high, low], axis=-1).reshape(count * levels, 2 * lats)
    moved = jnp.dot(both, shift, preferred_element_type=jnp.float32)
    moved = moved.reshape(count, levels, 2 * lats)
    y = (
        nc * x
        + nb * pltpu.roll(x, 1, 2)
        + nd * pltpu.roll(x, lats - 1, 2)
        + na * moved[..., :lats]
        + ne * moved[..., lats:]
    )
    mean = jnp.sum(share * y, axis=-2, keepdims=True)
    return y + cloud * mean


def step_kernel(
    tracer_devices,
    space_devices,
    x_hbm,
    codes_hbm,
    scales_hbm,
    slot_hbm,
    strength_hbm,
    top_hbm,
    emission_hbm,
    tag_hbm,
    out_ref,
    q0,
    q1,
    codes_ref,
    scales_ref,
    slot_ref,
    strength_ref,
    top_ref,
    emission_ref,
    tag_ref,
    pieces,
    staged,
    rows,
    met,
    coef,
    edge_coef,
    shift_ref,
    west_c,
    east_c,
    far_out,
    near_in,
    far_in,
    halo_out,
    halo_in,
    load_sem,
    piece_send,
    piece_recv,
    pass_send,
    pass_recv,
    west_send,
    west_recv,
    raw_send,
    raw_recv,
    halo_send,
    halo_recv,
):
    count, lons, levels, lats = x_hbm.shape
    last = lons - 1
    t_me = lax.axis_index("tracer")
    s_me = lax.axis_index("space")
    east = {"space": lax.rem(s_me + 1, space_devices)}
    west = {"space": lax.rem(s_me + space_devices - 1, space_devices)}
    toward = (east, west)
    sibling = {"tracer": t_me + 1 - 2 * lax.rem(t_me, CORES)}
    chips = tracer_devices // CORES
    block = count // BLOCKS

    def peer(k):
        return lax.rem(t_me + CORES * k, tracer_devices)

    small = (
        (codes_hbm, codes_ref),
        (scales_hbm, scales_ref),
        (tag_hbm, tag_ref),
        (emission_hbm, emission_ref),
        (slot_hbm, slot_ref),
        (strength_hbm, strength_ref),
        (top_hbm, top_ref),
    )
    loads = [
        pltpu.make_async_copy(src, dst, load_sem.at[n]) for n, (src, dst) in enumerate(small)
    ]
    cells = [
        pltpu.make_async_copy(x_hbm.at[:, lo:hi], q0.at[:, lo:hi], load_sem.at[len(small) + n])
        for n, (lo, hi) in enumerate(((0, 2), (lons - 2, lons), (2, lons - 2)))
    ]
    for copy in loads + cells:
        copy.start()

    barrier = pltpu.get_barrier_semaphore()
    for k in range(1, chips):
        pl.semaphore_signal(barrier, inc=1, device_id={"tracer": peer(k)}, device_id_type=MESH)
    for to in (sibling, east, west):
        pl.semaphore_signal(barrier, inc=1, device_id=to, device_id_type=MESH)

    staged[...] = jnp.zeros_like(staged)
    loads[0].wait()
    loads[1].wait()
    for r in range(codes_ref.shape[1]):
        staged[r * ROW_PITCH : r * ROW_PITCH + lons, :] = codes_ref[0, r].astype(jnp.float32)
        staged[r * ROW_PITCH + lons : r * ROW_PITCH + lons + 1, 0:lons] = scales_ref[
            0, r : r + 1, :
        ].astype(jnp.float32)
    pieces[t_me] = staged[...].astype(jnp.bfloat16)

    pl.semaphore_wait(barrier, chips - 1 + 3)

    def pass_on(k):
        held = pieces.at[peer(chips - k)]
        return pltpu.make_async_remote_copy(
            src_ref=held,
            dst_ref=held,
            send_sem=pass_send.at[k],
            recv_sem=pass_recv.at[k],
            device_id=sibling,
            device_id_type=MESH,
        )

    piece_copies = []
    for k in range(1, chips):
        copy = pltpu.make_async_remote_copy(
            src_ref=pieces.at[t_me],
            dst_ref=pieces.at[t_me],
            send_sem=piece_send.at[k],
            recv_sem=piece_recv.at[k],
            device_id={"tracer": peer(k)},
            device_id_type=MESH,
        )
        copy.start()
        piece_copies.append(copy)
    pass_on(0).start()

    for copy in loads[2:]:
        copy.wait()
    ids = t_me * count + lax.broadcasted_iota(jnp.int32, (count, 8, lats), 0)
    level_row = lax.broadcasted_iota(jnp.int32, (8, lats), 0)

    def emit(lon):
        tag = jnp.where(level_row == 0, tag_ref[pl.ds(lon, 1), :], -1)
        amount = jnp.broadcast_to(emission_ref[pl.ds(lon, 1), :], (8, lats))
        q0[:, lon, 0:8, :] += jnp.where(tag[None] == ids, amount[None], 0.0)

    def each_block(act):
        def one(blk, _):
            act(blk)
            return 0

        lax.fori_loop(0, BLOCKS, one, 0)

    def raw_copies(way, blk):
        part = pl.ds(blk * block, block)
        near = q0.at[part, last if way == EAST else 0]
        pairs = ((near, near_in.at[way, part]), (far_out.at[way, part], far_in.at[way, part]))
        return [
            pltpu.make_async_remote_copy(
                src_ref=src,
                dst_ref=dst,
                send_sem=raw_send.at[n, way, blk],
                recv_sem=raw_recv.at[n, way, blk],
                device_id=toward[way],
                device_id_type=MESH,
            )
            for n, (src, dst) in enumerate(pairs)
        ]

    cells[0].wait()
    cells[1].wait()
    for lon in (0, 1, last - 1, last):
        emit(lon)
    far_out[EAST] = q0[:, last - 1].astype(jnp.bfloat16)
    far_out[WEST] = q0[:, 1].astype(jnp.bfloat16)

    def first_sends(blk):
        for way in (EAST, WEST):
            for copy in raw_copies(way, blk):
                copy.start()

    each_block(first_sends)

    for k, copy in enumerate(piece_copies, 1):
        copy.wait_recv()
        pass_on(k).start()

    cells[2].wait()

    def emit_inside(n, _):
        emit(n + 2)
        return 0

    lax.fori_loop(0, lons - 4, emit_inside, 0)

    source = lax.broadcasted_iota(jnp.int32, (2 * lats, 2 * lats), 0) % lats
    target = lax.broadcasted_iota(jnp.int32, (2 * lats, 2 * lats), 1)
    wanted = jnp.where(target < lats, target - 2, target - lats + 2)
    shift_ref[...] = jnp.where(source == wanted, 1.0, 0.0).astype(jnp.bfloat16)

    for k in range(chips):
        pass_on(k).wait_recv()

    piece_count = slot_ref.shape[0]
    for j in range(piece_count):
        held = pieces[slot_ref[j]].astype(jnp.float32)
        rows[j * 3 * ROW_PITCH : (j + 1) * 3 * ROW_PITCH, :] = held[: 3 * ROW_PITCH]
    stack = 3 * piece_count
    scales = rows[pl.ds(lons, stack, stride=ROW_PITCH), :]

    def level_rows(lon):
        return rows[pl.ds(lon, stack, stride=ROW_PITCH), :] * scales[:, lon : lon + 1]

    met[last] = level_rows(last)
    east_c[...] = met[last, 0:levels, :]
    west_copy = pltpu.make_async_remote_copy(
        src_ref=east_c,
        dst_ref=west_c,
        send_sem=west_send,
        recv_sem=west_recv,
        device_id=east,
        device_id_type=MESH,
    )
    west_copy.start()
    for lon in range(last):
        met[lon] = level_rows(lon)

    lane = lax.broadcasted_iota(jnp.int32, (levels, lats), 1)
    level = lax.broadcasted_iota(jnp.int32, (levels, lats), 0)

    def east_parts(lon, before, here):
        la, lb, lc, ld = face_parts(before)
        ra, rb, rc, rd = face_parts(here)
        coef[lon, 0] = la
        coef[lon, 1] = lb - ra
        coef[lon, 2] = 1.0 + lc - rb
        coef[lon, 3] = ld - rc
        coef[lon, 4] = -rd

    def other_parts(lon):
        south = jnp.where(lane > 0, met[lon, levels : 2 * levels, :], 0.0)
        sa, sb, sc, sd = face_parts(south)
        ua, ub, uc, ud = (pltpu.roll(p, lats - 1, 1) for p in (sa, sb, sc, sd))
        air = 1.0 + 0.5 * met[lon, 2 * levels : 3 * levels, :]
        cloud = (level < top_ref[pl.ds(lon, 1), :]).astype(jnp.float32)
        strength = strength_ref[pl.ds(lon, 1), :]
        weighted = cloud * air
        mass = jnp.sum(weighted, axis=0, keepdims=True)
        keep = 1.0 - strength * cloud
        coef[lon, 5] = keep * jnp.where(lane > 1, sa, 0.0)
        coef[lon, 6] = keep * jnp.where(lane > 0, sb - ua, 0.0)
        coef[lon, 7] = keep * (1.0 + sc - ub)
        coef[lon, 8] = keep * jnp.where(lane < lats - 1, sd - uc, 0.0)
        coef[lon, 9] = keep * jnp.where(lane < lats - 2, -ud, 0.0)
        coef[lon, 10] = strength * weighted / (mass * keep)
        coef[lon, 11] = cloud

    group = 6

    def all_parts(n, _):
        for u in range(group):
            lon = n * group + u
            east_parts(lon, met[jnp.maximum(lon - 1, 0), 0:levels, :], met[lon, 0:levels, :])
            other_parts(lon)
        return 0

    lax.fori_loop(0, lons // group, all_parts, 0)

    shift = shift_ref[...]

    def inside(source, target, start, stop):
        def some(n, _):
            for u in range(PAIR):
                lon = start + n * PAIR + u
                parts = tuple(coef[lon, f] for f in range(FIELDS))
                around = [source[:, lon + d] for d in (-2, -1, 0, 1, 2)]
                target[:, lon] = column_step(around, parts, shift)
            return 0

        lax.fori_loop(0, (stop - start) // PAIR, some, 0)

    def edges(source, target, substep, blk):
        part = pl.ds(blk * block, block)

        def cell(place):
            if 0 <= place <= last:
                return source[part, place]
            way = EAST if place < 0 else WEST
            near = place in (-1, last + 1)
            if substep == 0:
                if near:
                    return near_in[way, part]
                return far_in[way, part].astype(jnp.float32)
            return halo_in[way, part, HIGH if near else LOW].astype(jnp.float32)

        for lon in (0, 1, last - 1, last):
            parts = [coef[lon, f] for f in range(FIELDS)]
            if substep == 1 and lon == 0:
                parts[0] = edge_coef[EAST]
            if substep == 1 and lon == last:
                parts[4] = edge_coef[WEST]
            around = [cell(lon + d) for d in (-2, -1, 0, 1, 2)]
            target[part, lon] = column_step(around, tuple(parts), shift)

    def halo_copy(way, blk):
        part = pl.ds(blk * block, block)
        return pltpu.make_async_remote_copy(
            src_ref=halo_out.at[way, part],
            dst_ref=halo_in.at[way, part],
            send_sem=halo_send.at[way, blk],
            recv_sem=halo_recv.at[way, blk],
            device_id=toward[way],
            device_id_type=MESH,
        )

    def stage(way, blk):
        part = pl.ds(blk * block, block)
        near, far = (last, last - 1) if way == EAST else (0, 1)
        bend = 0.25 * (1.0 - east_c[...]) if way == EAST else 0.25 * (1.0 + west_c[...])
        cell = q1[part, near]
        high = cell.astype(jnp.bfloat16)
        rest = (cell - high.astype(jnp.float32)) - bend * q1[part, far]
        halo_out[way, part, HIGH] = high
        halo_out[way, part, LOW] = rest.astype(jnp.bfloat16)

    middle = 2 + 6
    inside(q0, q1, 2, middle)

    west_copy.wait()
    east_parts(0, west_c[...], met[0, 0:levels, :])
    edge_coef[EAST] = jnp.maximum(west_c[...], 0.0)
    edge_coef[WEST] = -jnp.minimum(east_c[...], 0.0)

    def first_edges(blk):
        for way in (EAST, WEST):
            for copy in raw_copies(way, blk):
                copy.wait_recv()
        edges(q0, q1, 0, blk)
        for way in (EAST, WEST):
            stage(way, blk)
            halo_copy(way, blk).start()

    each_block(first_edges)
    inside(q0, q1, middle, lons - 2)
    inside(q1, out_ref, 2, lons - 2)

    def second_edges(blk):
        for way in (EAST, WEST):
            halo_copy(way, blk).wait_recv()
        edges(q1, out_ref, 1, blk)

    each_block(second_edges)

    def drain(blk):
        for way in (EAST, WEST):
            for copy in raw_copies(way, blk):
                copy.wait_send()
            halo_copy(way, blk).wait_send()

    each_block(drain)
    for copy in piece_copies:
        copy.wait_send()
    for k in range(chips):
        pass_on(k).wait_send()


def local(tracer_devices, space_devices, tracers, met_codes, met_scales, owner_slot, conv_weight,
          cloud_top, emission, region_tag):
    by_lon = jnp.transpose(tracers, (0, 2, 1, 3))
    count, lons, levels, lats = by_lon.shape
    pieces = owner_slot.shape[0]
    stack = pieces * met_codes.shape[1]
    chips = tracer_devices // CORES
    side = (2, count, levels, lats)
    halo = (2, count, 2, levels, lats)
    hbm = pl.BlockSpec(memory_space=pltpu.HBM)
    dma = pltpu.SemaphoreType.DMA
    out = pl.pallas_call(
        functools.partial(step_kernel, tracer_devices, space_devices),
        out_shape=jax.ShapeDtypeStruct(by_lon.shape, jnp.float32),
        in_specs=[hbm] * 8,
        out_specs=pl.BlockSpec(memory_space=pltpu.VMEM),
        scratch_shapes=[
            pltpu.VMEM(by_lon.shape, jnp.float32),
            pltpu.VMEM(by_lon.shape, jnp.float32),
            pltpu.VMEM(met_codes.shape, jnp.bfloat16),
            pltpu.VMEM(met_scales.shape, jnp.bfloat16),
            pltpu.SMEM(owner_slot.shape, jnp.int32),
            pltpu.VMEM(conv_weight.shape, jnp.float32),
            pltpu.VMEM(cloud_top.shape, jnp.int32),
            pltpu.VMEM(emission.shape, jnp.float32),
            pltpu.VMEM(region_tag.shape, jnp.int32),
            pltpu.VMEM((pieces, PIECE_ROWS, lats), jnp.bfloat16),
            pltpu.VMEM((PIECE_ROWS, lats), jnp.float32),
            pltpu.VMEM((pieces * 3 * ROW_PITCH, lats), jnp.float32),
            pltpu.VMEM((lons, stack, lats), jnp.float32),
            pltpu.VMEM((lons, FIELDS, levels, lats), jnp.float32),
            pltpu.VMEM((2, levels, lats), jnp.float32),
            pltpu.VMEM((2 * lats, 2 * lats), jnp.bfloat16),
            pltpu.VMEM((levels, lats), jnp.float32),
            pltpu.VMEM((levels, lats), jnp.float32),
            pltpu.VMEM(side, jnp.bfloat16),
            pltpu.VMEM(side, jnp.float32),
            pltpu.VMEM(side, jnp.bfloat16),
            pltpu.VMEM(halo, jnp.bfloat16),
            pltpu.VMEM(halo, jnp.bfloat16),
            dma((10,)),
            dma((chips,)),
            dma((chips,)),
            dma((chips,)),
            dma((chips,)),
            dma,
            dma,
            dma((2, 2, BLOCKS)),
            dma((2, 2, BLOCKS)),
            dma((2, BLOCKS)),
            dma((2, BLOCKS)),
        ],
        compiler_params=pltpu.CompilerParams(
            collective_id=0, has_side_effects=True, vmem_limit_bytes=48 * 1024 * 1024
        ),
        name="transport_step",
    )(
        *(
            pltpu.with_memory_space_constraint(x, pltpu.HBM)
            for x in (by_lon, met_codes, met_scales, owner_slot, conv_weight, cloud_top, emission)
            + (region_tag,)
        )
    )
    return jnp.transpose(out, (0, 2, 1, 3))


def solution(mesh):
    placed = (
        P("tracer", None, "space", None),
        P("tracer", None, "space", None),
        P("tracer", None, "space"),
        P(),
        P("space", None),
        P("space", None),
        P("space", None),
        P("space", None),
    )
    return jax.shard_map(
        functools.partial(local, mesh.shape["tracer"], mesh.shape["space"]),
        mesh=mesh,
        in_specs=placed,
        out_specs=P("tracer", None, "space", None),
        check_vma=False,
    )
```

```python
import functools

import jax
import jax.numpy as jnp
from jax import lax
from jax.experimental import pallas as pl
from jax.experimental.pallas import tpu as pltpu
from jax.sharding import PartitionSpec as P

MESH = pl.DeviceIdType.MESH
EAST, WEST = 0, 1
HIGH, LOW = 0, 1
NEAR, FAR = 0, 1
BLOCKS = 4
DIRECT = 5
STEPS = 1200.0
FLOOR = 24.0
ROW = 4
FIELDS = 12
ROW_PITCH = 24
PIECE_ROWS = 80
CORES = 2
PAIR = 2


def face_parts(c):
    size = jnp.abs(c)
    bend = 0.25 * size * (1.0 - size)
    up = c > 0
    zero = jnp.zeros_like(c)
    return (
        jnp.where(up, -bend, zero),
        jnp.where(up, c, -bend),
        jnp.where(up, bend, c),
        jnp.where(up, zero, bend),
    )


def encoded(value):
    size = jnp.maximum(jnp.abs(value), 2.0**-FLOOR)
    steps = jnp.log2(size) * STEPS + (FLOOR * STEPS + 0.5)
    steps = jnp.where(value < 0, -steps, steps)
    return steps.astype(jnp.int32).astype(jnp.int16)


def decoded(code):
    steps = code.astype(jnp.int32).astype(jnp.float32)
    size = jnp.exp2(jnp.abs(steps) * (1.0 / STEPS) - FLOOR)
    return jnp.where(steps < 0, -size, size)


def column_step(cells, parts, shift):
    ea, eb, ec, ed, ee, na, nb, nc, nd, ne, share, cloud = parts
    x = ea * cells[0] + eb * cells[1] + ec * cells[2] + ed * cells[3] + ee * cells[4]
    count, levels, lats = x.shape
    high = x.astype(jnp.bfloat16)
    low = (x - high.astype(jnp.float32)).astype(jnp.bfloat16)
    both = jnp.concatenate([high, low], axis=-1).reshape(count * levels, 2 * lats)
    moved = jnp.dot(both, shift, preferred_element_type=jnp.float32)
    moved = moved.reshape(count, levels, 2 * lats)
    y = (
        nc * x
        + nb * pltpu.roll(x, 1, 2)
        + nd * pltpu.roll(x, lats - 1, 2)
        + na * moved[..., :lats]
        + ne * moved[..., lats:]
    )
    mean = jnp.sum(share * y, axis=-2, keepdims=True)
    return y + cloud * mean


def step_kernel(
    tracer_devices,
    space_devices,
    x_hbm,
    codes_hbm,
    scales_hbm,
    slot_hbm,
    strength_hbm,
    top_hbm,
    emission_hbm,
    tag_hbm,
    out_ref,
    q0,
    q1,
    codes_ref,
    scales_ref,
    slot_ref,
    strength_ref,
    top_ref,
    emission_ref,
    tag_ref,
    pieces,
    staged,
    rows,
    met,
    coef,
    edge_coef,
    shift_ref,
    west_c,
    east_c,
    raw_out,
    raw_in,
    raw_relay,
    halo_out,
    halo_in,
    halo_relay,
    load_sem,
    piece_send,
    piece_recv,
    pass_send,
    pass_recv,
    west_send,
    west_recv,
    raw_sems,
    raw_relay_sems,
    halo_sems,
    halo_relay_sems,
):
    count, lons, levels, lats = x_hbm.shape
    last = lons - 1
    t_me = lax.axis_index("tracer")
    s_me = lax.axis_index("space")
    east = {"space": lax.rem(s_me + 1, space_devices)}
    west = {"space": lax.rem(s_me + space_devices - 1, space_devices)}
    toward = (east, west)
    place = lax.rem(s_me, ROW)
    ends = (place == ROW - 1, place == 0)
    edge = jnp.logical_or(ends[EAST], ends[WEST])

    def along(step):
        return {"space": lax.rem(s_me + step + space_devices, space_devices)}

    hop = (along(1 - ROW), along(ROW - 1))
    relay_way = jnp.where(ends[WEST], EAST, WEST)
    onward = along(jnp.where(ends[WEST], ROW, -ROW))
    sibling = {"tracer": t_me + 1 - 2 * lax.rem(t_me, CORES)}
    chips = tracer_devices // CORES
    block = count // BLOCKS

    def peer(k):
        return lax.rem(t_me + CORES * k, tracer_devices)

    small = (
        (codes_hbm, codes_ref),
        (scales_hbm, scales_ref),
        (tag_hbm, tag_ref),
        (emission_hbm, emission_ref),
        (slot_hbm, slot_ref),
        (strength_hbm, strength_ref),
        (top_hbm, top_ref),
    )
    loads = [
        pltpu.make_async_copy(src, dst, load_sem.at[n]) for n, (src, dst) in enumerate(small)
    ]
    cells = [
        pltpu.make_async_copy(x_hbm.at[:, lo:hi], q0.at[:, lo:hi], load_sem.at[len(small) + n])
        for n, (lo, hi) in enumerate(((0, 2), (lons - 2, lons), (2, lons - 2)))
    ]
    for copy in loads + cells:
        copy.start()

    barrier = pltpu.get_barrier_semaphore()
    for k in range(1, chips):
        pl.semaphore_signal(barrier, inc=1, device_id={"tracer": peer(k)}, device_id_type=MESH)
    for to in (sibling, east, west):
        pl.semaphore_signal(barrier, inc=1, device_id=to, device_id_type=MESH)

    @pl.when(edge)
    def _():
        other = along(jnp.where(ends[WEST], ROW - 1, 1 - ROW))
        for to in (other, along(ROW), along(-ROW)):
            pl.semaphore_signal(barrier, inc=1, device_id=to, device_id_type=MESH)

    staged[...] = jnp.zeros_like(staged)
    loads[0].wait()
    loads[1].wait()
    for r in range(codes_ref.shape[1]):
        staged[r * ROW_PITCH : r * ROW_PITCH + lons, :] = codes_ref[0, r].astype(jnp.float32)
        staged[r * ROW_PITCH + lons : r * ROW_PITCH + lons + 1, 0:lons] = scales_ref[
            0, r : r + 1, :
        ].astype(jnp.float32)
    pieces[t_me] = staged[...].astype(jnp.bfloat16)

    pl.semaphore_wait(barrier, chips - 1 + 3 + jnp.where(edge, 3, 0))

    def pass_on(k):
        held = pieces.at[peer(chips - k)]
        return pltpu.make_async_remote_copy(
            src_ref=held,
            dst_ref=held,
            send_sem=pass_send.at[k],
            recv_sem=pass_recv.at[k],
            device_id=sibling,
            device_id_type=MESH,
        )

    piece_copies = []
    for k in range(1, chips):
        copy = pltpu.make_async_remote_copy(
            src_ref=pieces.at[t_me],
            dst_ref=pieces.at[t_me],
            send_sem=piece_send.at[k],
            recv_sem=piece_recv.at[k],
            device_id={"tracer": peer(k)},
            device_id_type=MESH,
        )
        copy.start()
        piece_copies.append(copy)
    pass_on(0).start()

    for copy in loads[2:]:
        copy.wait()
    ids = t_me * count + lax.broadcasted_iota(jnp.int32, (count, 8, lats), 0)
    level_row = lax.broadcasted_iota(jnp.int32, (8, lats), 0)

    def emit(lon):
        tag = jnp.where(level_row == 0, tag_ref[pl.ds(lon, 1), :], -1)
        amount = jnp.broadcast_to(emission_ref[pl.ds(lon, 1), :], (8, lats))
        q0[:, lon, 0:8, :] += jnp.where(tag[None] == ids, amount[None], 0.0)

    def each_block(act):
        def one(blk, _):
            act(blk)
            return 0

        lax.fori_loop(0, BLOCKS, one, 0)

    def exchange(out, into, relay, sems, relay_sems):
        def halves(blk):
            start = blk * block
            return pl.ds(start, DIRECT), pl.ds(start + DIRECT, block - DIRECT)

        def straight(way, blk, n):
            part = halves(blk)[n]
            return pltpu.make_async_remote_copy(
                src_ref=out.at[way, part],
                dst_ref=into.at[way, part],
                send_sem=sems.at[0, way, blk, n],
                recv_sem=sems.at[1, way, blk, n],
                device_id=toward[way],
                device_id_type=MESH,
            )

        def detour(way, blk):
            part = halves(blk)[1]
            return pltpu.make_async_remote_copy(
                src_ref=out.at[way, part],
                dst_ref=relay.at[part],
                send_sem=sems.at[0, way, blk, 1],
                recv_sem=relay_sems.at[1, blk],
                device_id=hop[way],
                device_id_type=MESH,
            )

        def second_leg(blk):
            part = halves(blk)[1]
            return pltpu.make_async_remote_copy(
                src_ref=relay.at[part],
                dst_ref=into.at[relay_way, part],
                send_sem=relay_sems.at[0, blk],
                recv_sem=sems.at[1, relay_way, blk, 1],
                device_id=onward,
                device_id_type=MESH,
            )

        def start_relayed(blk):
            for way in (EAST, WEST):

                @pl.when(ends[way])
                def _(way=way):
                    detour(way, blk).start()

                @pl.when(jnp.logical_not(ends[way]))
                def _(way=way):
                    straight(way, blk, 1).start()

        def start_direct(blk):
            for way in (EAST, WEST):
                straight(way, blk, 0).start()

        def forward(blk):
            @pl.when(edge)
            def _():
                detour(EAST, blk).wait_recv()
                second_leg(blk).start()

        def receive(blk):
            for way in (EAST, WEST):
                for n in (0, 1):
                    straight(way, blk, n).wait_recv()

        def drain(blk):
            for way in (EAST, WEST):
                for n in (0, 1):
                    straight(way, blk, n).wait_send()

            @pl.when(edge)
            def _():
                second_leg(blk).wait_send()

        return start_relayed, start_direct, forward, receive, drain

    raw = exchange(raw_out, raw_in, raw_relay, raw_sems, raw_relay_sems)
    halo = exchange(halo_out, halo_in, halo_relay, halo_sems, halo_relay_sems)
    RELAYED, STRAIGHT, FORWARD, RECEIVE, DRAIN = range(5)

    cells[0].wait()
    cells[1].wait()
    for lon in (0, 1, last - 1, last):
        emit(lon)
    def first_sends(blk):
        part = pl.ds(blk * block, block)
        for way, near, far in ((EAST, last, last - 1), (WEST, 0, 1)):
            raw_out[way, part, NEAR] = encoded(q0[part, near])
            raw_out[way, part, FAR] = encoded(q0[part, far])
        raw[RELAYED](blk)
        raw[STRAIGHT](blk)

    each_block(first_sends)

    cells[2].wait()

    def emit_inside(n, _):
        emit(n + 2)
        return 0

    lax.fori_loop(0, lons - 4, emit_inside, 0)
    raw[FORWARD](0)

    for k, copy in enumerate(piece_copies, 1):
        copy.wait_recv()
        pass_on(k).start()
    raw[FORWARD](1)
    raw[FORWARD](2)

    source = lax.broadcasted_iota(jnp.int32, (2 * lats, 2 * lats), 0) % lats
    target = lax.broadcasted_iota(jnp.int32, (2 * lats, 2 * lats), 1)
    wanted = jnp.where(target < lats, target - 2, target - lats + 2)
    shift_ref[...] = jnp.where(source == wanted, 1.0, 0.0).astype(jnp.bfloat16)

    for k in range(chips):
        pass_on(k).wait_recv()

    piece_count = slot_ref.shape[0]
    for j in range(piece_count):
        held = pieces[slot_ref[j]].astype(jnp.float32)
        rows[j * 3 * ROW_PITCH : (j + 1) * 3 * ROW_PITCH, :] = held[: 3 * ROW_PITCH]
    stack = 3 * piece_count
    scales = rows[pl.ds(lons, stack, stride=ROW_PITCH), :]

    def level_rows(lon):
        return rows[pl.ds(lon, stack, stride=ROW_PITCH), :] * scales[:, lon : lon + 1]

    met[last] = level_rows(last)
    east_c[...] = met[last, 0:levels, :]
    west_copy = pltpu.make_async_remote_copy(
        src_ref=east_c,
        dst_ref=west_c,
        send_sem=west_send,
        recv_sem=west_recv,
        device_id=east,
        device_id_type=MESH,
    )
    west_copy.start()
    raw[FORWARD](3)
    for lon in range(last):
        met[lon] = level_rows(lon)

    lane = lax.broadcasted_iota(jnp.int32, (levels, lats), 1)
    level = lax.broadcasted_iota(jnp.int32, (levels, lats), 0)

    def east_parts(lon, before, here):
        la, lb, lc, ld = face_parts(before)
        ra, rb, rc, rd = face_parts(here)
        coef[lon, 0] = la
        coef[lon, 1] = lb - ra
        coef[lon, 2] = 1.0 + lc - rb
        coef[lon, 3] = ld - rc
        coef[lon, 4] = -rd

    def other_parts(lon):
        south = jnp.where(lane > 0, met[lon, levels : 2 * levels, :], 0.0)
        sa, sb, sc, sd = face_parts(south)
        ua, ub, uc, ud = (pltpu.roll(p, lats - 1, 1) for p in (sa, sb, sc, sd))
        air = 1.0 + 0.5 * met[lon, 2 * levels : 3 * levels, :]
        cloud = (level < top_ref[pl.ds(lon, 1), :]).astype(jnp.float32)
        strength = strength_ref[pl.ds(lon, 1), :]
        weighted = cloud * air
        mass = jnp.sum(weighted, axis=0, keepdims=True)
        keep = 1.0 - strength * cloud
        coef[lon, 5] = keep * jnp.where(lane > 1, sa, 0.0)
        coef[lon, 6] = keep * jnp.where(lane > 0, sb - ua, 0.0)
        coef[lon, 7] = keep * (1.0 + sc - ub)
        coef[lon, 8] = keep * jnp.where(lane < lats - 1, sd - uc, 0.0)
        coef[lon, 9] = keep * jnp.where(lane < lats - 2, -ud, 0.0)
        coef[lon, 10] = strength * weighted / (mass * keep)
        coef[lon, 11] = cloud

    group = 6

    def all_parts(n, _):
        for u in range(group):
            lon = n * group + u
            east_parts(lon, met[jnp.maximum(lon - 1, 0), 0:levels, :], met[lon, 0:levels, :])
            other_parts(lon)
        return 0

    lax.fori_loop(0, lons // group, all_parts, 0)

    shift = shift_ref[...]

    def inside(source, target, start, stop):
        def some(n, _):
            for u in range(PAIR):
                lon = start + n * PAIR + u
                parts = tuple(coef[lon, f] for f in range(FIELDS))
                around = [source[:, lon + d] for d in (-2, -1, 0, 1, 2)]
                target[:, lon] = column_step(around, parts, shift)
            return 0

        lax.fori_loop(0, (stop - start) // PAIR, some, 0)

    def edges(source, target, substep, blk):
        part = pl.ds(blk * block, block)

        def cell(place):
            if 0 <= place <= last:
                return source[part, place]
            way = EAST if place < 0 else WEST
            near = place in (-1, last + 1)
            if substep == 1:
                return halo_in[way, part, HIGH if near else LOW].astype(jnp.float32)
            return decoded(raw_in[way, part, NEAR if near else FAR])

        for lon in (0, 1, last - 1, last):
            parts = [coef[lon, f] for f in range(FIELDS)]
            if substep == 1 and lon == 0:
                parts[0] = edge_coef[EAST]
            if substep == 1 and lon == last:
                parts[4] = edge_coef[WEST]
            around = [cell(lon + d) for d in (-2, -1, 0, 1, 2)]
            target[part, lon] = column_step(around, tuple(parts), shift)

    def stage(way, blk):
        part = pl.ds(blk * block, block)
        near, far = (last, last - 1) if way == EAST else (0, 1)
        bend = 0.25 * (1.0 - east_c[...]) if way == EAST else 0.25 * (1.0 + west_c[...])
        cell = q1[part, near]
        high = cell.astype(jnp.bfloat16)
        rest = (cell - high.astype(jnp.float32)) - bend * q1[part, far]
        halo_out[way, part, HIGH] = high
        halo_out[way, part, LOW] = rest.astype(jnp.bfloat16)

    west_copy.wait()
    east_parts(0, west_c[...], met[0, 0:levels, :])
    edge_coef[EAST] = jnp.maximum(west_c[...], 0.0)
    edge_coef[WEST] = -jnp.minimum(east_c[...], 0.0)

    def first_edges(blk):
        raw[RECEIVE](blk)
        edges(q0, q1, 0, blk)
        for way in (EAST, WEST):
            stage(way, blk)
        halo[RELAYED](blk)
        halo[STRAIGHT](blk)

    inside_stops = (2, 4, 8, 12, 16)
    for blk in range(BLOCKS):
        first_edges(blk)
        if blk:
            halo[FORWARD](blk - 1)
        inside(q0, q1, inside_stops[blk], inside_stops[blk + 1])

    halves = 2 + 4
    inside(q1, out_ref, 2, halves)
    halo[FORWARD](BLOCKS - 1)
    inside(q1, out_ref, halves, lons - 2)

    def second_edges(blk):
        halo[RECEIVE](blk)
        edges(q1, out_ref, 1, blk)

    each_block(second_edges)
    each_block(raw[DRAIN])
    each_block(halo[DRAIN])
    for copy in piece_copies:
        copy.wait_send()
    for k in range(chips):
        pass_on(k).wait_send()


def local(tracer_devices, space_devices, tracers, met_codes, met_scales, owner_slot, conv_weight,
          cloud_top, emission, region_tag):
    by_lon = jnp.transpose(tracers, (0, 2, 1, 3))
    count, lons, levels, lats = by_lon.shape
    pieces = owner_slot.shape[0]
    stack = pieces * met_codes.shape[1]
    chips = tracer_devices // CORES
    halo = (count, 2, levels, lats)
    hbm = pl.BlockSpec(memory_space=pltpu.HBM)
    dma = pltpu.SemaphoreType.DMA
    out = pl.pallas_call(
        functools.partial(step_kernel, tracer_devices, space_devices),
        out_shape=jax.ShapeDtypeStruct(by_lon.shape, jnp.float32),
        in_specs=[hbm] * 8,
        out_specs=pl.BlockSpec(memory_space=pltpu.VMEM),
        scratch_shapes=[
            pltpu.VMEM(by_lon.shape, jnp.float32),
            pltpu.VMEM(by_lon.shape, jnp.float32),
            pltpu.VMEM(met_codes.shape, jnp.bfloat16),
            pltpu.VMEM(met_scales.shape, jnp.bfloat16),
            pltpu.SMEM(owner_slot.shape, jnp.int32),
            pltpu.VMEM(conv_weight.shape, jnp.float32),
            pltpu.VMEM(cloud_top.shape, jnp.int32),
            pltpu.VMEM(emission.shape, jnp.float32),
            pltpu.VMEM(region_tag.shape, jnp.int32),
            pltpu.VMEM((pieces, PIECE_ROWS, lats), jnp.bfloat16),
            pltpu.VMEM((PIECE_ROWS, lats), jnp.float32),
            pltpu.VMEM((pieces * 3 * ROW_PITCH, lats), jnp.float32),
            pltpu.VMEM((lons, stack, lats), jnp.float32),
            pltpu.VMEM((lons, FIELDS, levels, lats), jnp.float32),
            pltpu.VMEM((2, levels, lats), jnp.float32),
            pltpu.VMEM((2 * lats, 2 * lats), jnp.bfloat16),
            pltpu.VMEM((levels, lats), jnp.float32),
            pltpu.VMEM((levels, lats), jnp.float32),
            pltpu.VMEM((2,) + halo, jnp.int16),
            pltpu.VMEM((2,) + halo, jnp.int16),
            pltpu.VMEM(halo, jnp.int16),
            pltpu.VMEM((2,) + halo, jnp.bfloat16),
            pltpu.VMEM((2,) + halo, jnp.bfloat16),
            pltpu.VMEM(halo, jnp.bfloat16),
            dma((10,)),
            dma((chips,)),
            dma((chips,)),
            dma((chips,)),
            dma((chips,)),
            dma,
            dma,
            dma((2, 2, BLOCKS, 2)),
            dma((2, BLOCKS)),
            dma((2, 2, BLOCKS, 2)),
            dma((2, BLOCKS)),
        ],
        compiler_params=pltpu.CompilerParams(
            collective_id=0, has_side_effects=True, vmem_limit_bytes=48 * 1024 * 1024
        ),
        name="transport_step",
    )(
        *(
            pltpu.with_memory_space_constraint(x, pltpu.HBM)
            for x in (by_lon, met_codes, met_scales, owner_slot, conv_weight, cloud_top, emission)
            + (region_tag,)
        )
    )
    return jnp.transpose(out, (0, 2, 1, 3))


def solution(mesh):
    placed = (
        P("tracer", None, "space", None),
        P("tracer", None, "space", None),
        P("tracer", None, "space"),
        P(),
        P("space", None),
        P("space", None),
        P("space", None),
        P("space", None),
    )
    return jax.shard_map(
        functools.partial(local, mesh.shape["tracer"], mesh.shape["space"]),
        mesh=mesh,
        in_specs=placed,
        out_specs=P("tracer", None, "space", None),
        check_vma=False,
    )
```

```python
import functools

import jax
import jax.numpy as jnp
from jax import lax
from jax.experimental import pallas as pl
from jax.experimental.pallas import tpu as pltpu
from jax.sharding import PartitionSpec as P

MESH = pl.DeviceIdType.MESH
EAST, WEST = 0, 1
NEAR, FAR = 0, 1
RIM = 2
BLOCKS = 4
DIRECT = (5, 4)
STEPS = 1200.0
FLOOR = 24.0
ROW = 4
FIELDS = 12
ROW_GROUP = 16
CORES = 2
PAIR = 2


def face_parts(c):
    size = jnp.abs(c)
    bend = 0.25 * size * (1.0 - size)
    up = c > 0
    zero = jnp.zeros_like(c)
    return (
        jnp.where(up, -bend, zero),
        jnp.where(up, c, -bend),
        jnp.where(up, bend, c),
        jnp.where(up, zero, bend),
    )


def encoded(value):
    size = jnp.maximum(jnp.abs(value), 2.0**-FLOOR)
    steps = jnp.log2(size) * STEPS + (FLOOR * STEPS + 0.5)
    steps = jnp.where(value < 0, -steps, steps)
    return steps.astype(jnp.int32).astype(jnp.int16)


def decoded(code):
    steps = code.astype(jnp.int32).astype(jnp.float32)
    size = jnp.exp2(jnp.abs(steps) * (1.0 / STEPS) - FLOOR)
    return jnp.where(steps < 0, -size, size)


def column_step(cells, parts, shift):
    ea, eb, ec, ed, ee, na, nb, nc, nd, ne, share, cloud = parts
    x = ea * cells[0] + eb * cells[1] + ec * cells[2] + ed * cells[3] + ee * cells[4]
    count, levels, lats = x.shape
    high = x.astype(jnp.bfloat16)
    low = (x - high.astype(jnp.float32)).astype(jnp.bfloat16)
    both = jnp.concatenate([high, low], axis=-1).reshape(count * levels, 2 * lats)
    moved = jnp.dot(both, shift, preferred_element_type=jnp.float32)
    moved = moved.reshape(count, levels, 2 * lats)
    y = (
        nc * x
        + nb * pltpu.roll(x, 1, 2)
        + nd * pltpu.roll(x, lats - 1, 2)
        + na * moved[..., :lats]
        + ne * moved[..., lats:]
    )
    mean = jnp.sum(share * y, axis=-2, keepdims=True)
    return y + cloud * mean


def step_kernel(
    tracer_devices,
    space_devices,
    x_hbm,
    codes_hbm,
    scales_hbm,
    slot_hbm,
    strength_hbm,
    top_hbm,
    emission_hbm,
    tag_hbm,
    out_ref,
    q0,
    q1,
    codes_ref,
    scales_ref,
    slot_ref,
    strength_ref,
    top_ref,
    emission_ref,
    tag_ref,
    pieces,
    staged,
    rows,
    met,
    coef,
    shift_ref,
    sky_out,
    sky_in,
    wing_out,
    wing_in,
    wave_out,
    wave_in,
    wave_relay,
    load_sem,
    piece_send,
    piece_recv,
    pass_send,
    pass_recv,
    sky_sems,
    wing_sems,
    wave_sems,
    relay_sems,
):
    count, lons, levels, lats = x_hbm.shape
    last = lons - 1
    t_me = lax.axis_index("tracer")
    s_me = lax.axis_index("space")
    east = {"space": lax.rem(s_me + 1, space_devices)}
    west = {"space": lax.rem(s_me + space_devices - 1, space_devices)}
    toward = (east, west)
    place = lax.rem(s_me, ROW)
    ends = (place == ROW - 1, place == 0)
    edge = jnp.logical_or(ends[EAST], ends[WEST])

    def along(step):
        return {"space": lax.rem(s_me + step + space_devices, space_devices)}

    hop = (along(1 - ROW), along(ROW - 1))
    relay_way = jnp.where(ends[WEST], EAST, WEST)
    onward = along(jnp.where(ends[WEST], ROW, -ROW))
    sibling = {"tracer": t_me + 1 - 2 * lax.rem(t_me, CORES)}
    chips = tracer_devices // CORES
    block = count // BLOCKS
    level_rows = codes_hbm.shape[1]
    pitch = lons + 1
    piece_rows = level_rows * pitch

    def in_q0(lon):
        return lon + 2 * RIM

    def in_q1(lon):
        return lon + RIM

    def in_met(lon):
        return lon + RIM + 1

    def peer(k):
        return lax.rem(t_me + CORES * k, tracer_devices)

    small = (
        (codes_hbm, codes_ref),
        (scales_hbm, scales_ref),
        (tag_hbm, tag_ref),
        (emission_hbm, emission_ref),
        (slot_hbm, slot_ref),
        (strength_hbm, strength_ref),
        (top_hbm, top_ref),
    )
    loads = [
        pltpu.make_async_copy(src, dst, load_sem.at[n]) for n, (src, dst) in enumerate(small)
    ]
    rims = ((0, 2 * RIM), (lons - 2 * RIM, lons), (2 * RIM, lons - 2 * RIM))
    cells = [
        pltpu.make_async_copy(
            x_hbm.at[:, lo:hi], q0.at[:, in_q0(lo) : in_q0(hi)], load_sem.at[len(small) + n]
        )
        for n, (lo, hi) in enumerate(rims)
    ]
    for copy in loads + cells:
        copy.start()

    barrier = pltpu.get_barrier_semaphore()
    for k in range(1, chips):
        pl.semaphore_signal(barrier, inc=1, device_id={"tracer": peer(k)}, device_id_type=MESH)
    for to in (sibling, east, west):
        pl.semaphore_signal(barrier, inc=1, device_id=to, device_id_type=MESH)

    @pl.when(edge)
    def _():
        other = along(jnp.where(ends[WEST], ROW - 1, 1 - ROW))
        for to in (other, along(ROW), along(-ROW)):
            pl.semaphore_signal(barrier, inc=1, device_id=to, device_id_type=MESH)

    staged[...] = jnp.zeros_like(staged)
    loads[0].wait()
    loads[1].wait()
    for r in range(level_rows):
        at = r * pitch
        staged[at : at + lons, :] = codes_ref[0, r].astype(jnp.float32)
        staged[at + lons : at + lons + 1, 0:lons] = scales_ref[0, r : r + 1, :].astype(jnp.float32)
    pieces[t_me] = staged[...].astype(jnp.bfloat16)

    pl.semaphore_wait(barrier, chips - 1 + 3 + jnp.where(edge, 3, 0))

    def pass_on(k):
        held = pieces.at[peer(chips - k)]
        return pltpu.make_async_remote_copy(
            src_ref=held,
            dst_ref=held,
            send_sem=pass_send.at[k],
            recv_sem=pass_recv.at[k],
            device_id=sibling,
            device_id_type=MESH,
        )

    piece_copies = []
    for k in range(1, chips):
        copy = pltpu.make_async_remote_copy(
            src_ref=pieces.at[t_me],
            dst_ref=pieces.at[t_me],
            send_sem=piece_send.at[k],
            recv_sem=piece_recv.at[k],
            device_id={"tracer": peer(k)},
            device_id_type=MESH,
        )
        copy.start()
        piece_copies.append(copy)
    pass_on(0).start()

    for copy in loads[2:]:
        copy.wait()
    ids = t_me * count + lax.broadcasted_iota(jnp.int32, (count, 8, lats), 0)
    level_row = lax.broadcasted_iota(jnp.int32, (8, lats), 0)

    def emit(lon):
        tag = jnp.where(level_row == 0, tag_ref[pl.ds(lon, 1), :], -1)
        amount = jnp.broadcast_to(emission_ref[pl.ds(lon, 1), :], (8, lats))
        q0[:, in_q0(lon), 0:8, :] += jnp.where(tag[None] == ids, amount[None], 0.0)

    def each_block(act):
        def one(blk, _):
            act(blk)
            return 0

        lax.fori_loop(0, BLOCKS, one, 0)

    def wave(n):
        out, into, relay = wave_out.at[n], wave_in.at[n], wave_relay.at[n]

        def halves(blk):
            start = blk * block
            return pl.ds(start, DIRECT[n]), pl.ds(start + DIRECT[n], block - DIRECT[n])

        def straight(way, blk, h):
            part = halves(blk)[h]
            return pltpu.make_async_remote_copy(
                src_ref=out.at[way, part],
                dst_ref=into.at[way, part],
                send_sem=wave_sems.at[n, 0, way, blk, h],
                recv_sem=wave_sems.at[n, 1, way, blk, h],
                device_id=toward[way],
                device_id_type=MESH,
            )

        def detour(way, blk):
            part = halves(blk)[1]
            return pltpu.make_async_remote_copy(
                src_ref=out.at[way, part],
                dst_ref=relay.at[part],
                send_sem=wave_sems.at[n, 0, way, blk, 1],
                recv_sem=relay_sems.at[n, 1, blk],
                device_id=hop[way],
                device_id_type=MESH,
            )

        def second_leg(blk):
            part = halves(blk)[1]
            return pltpu.make_async_remote_copy(
                src_ref=relay.at[part],
                dst_ref=into.at[relay_way, part],
                send_sem=relay_sems.at[n, 0, blk],
                recv_sem=wave_sems.at[n, 1, relay_way, blk, 1],
                device_id=onward,
                device_id_type=MESH,
            )

        def send(blk):
            part = pl.ds(blk * block, block)
            for way in (EAST, WEST):
                for slot in (NEAR, FAR):
                    depth = 2 * n + slot
                    lon = last - depth if way == EAST else depth
                    out[way, part, slot] = encoded(q0[part, in_q0(lon)])
            for way in (EAST, WEST):

                @pl.when(ends[way])
                def _(way=way):
                    detour(way, blk).start()

                @pl.when(jnp.logical_not(ends[way]))
                def _(way=way):
                    straight(way, blk, 1).start()

            for way in (EAST, WEST):
                straight(way, blk, 0).start()

        def forward(blk):
            @pl.when(edge)
            def _():
                detour(EAST, blk).wait_recv()
                second_leg(blk).start()

        def receive(blk):
            part = pl.ds(blk * block, block)
            for way in (EAST, WEST):
                for h in (0, 1):
                    straight(way, blk, h).wait_recv()
                for slot in (NEAR, FAR):
                    depth = 2 * n + slot
                    lon = -1 - depth if way == EAST else lons + depth
                    q0[part, in_q0(lon)] = decoded(into[way, part, slot])

        def drain(blk):
            for way in (EAST, WEST):
                for h in (0, 1):
                    straight(way, blk, h).wait_send()

            @pl.when(edge)
            def _():
                second_leg(blk).wait_send()

        return send, forward, receive, drain

    waves = (wave(0), wave(1))
    SEND, FORWARD, RECEIVE, DRAIN = range(4)

    cells[0].wait()
    cells[1].wait()
    for lon in (0, 1, last - 1, last):
        emit(lon)
    each_block(waves[0][SEND])
    for lon in (2, 3, last - 3, last - 2):
        emit(lon)
    each_block(waves[1][SEND])

    def sky_copy(way):
        return pltpu.make_async_remote_copy(
            src_ref=sky_out.at[way],
            dst_ref=sky_in.at[way],
            send_sem=sky_sems.at[0, way],
            recv_sem=sky_sems.at[1, way],
            device_id=toward[way],
            device_id_type=MESH,
        )

    sky_out[...] = jnp.zeros_like(sky_out)
    for way in (EAST, WEST):
        for slot in (NEAR, FAR):
            lon = last - slot if way == EAST else slot
            sky_out[way, slot : slot + 1, :] = strength_ref[lon : lon + 1, :]
            sky_out[way, RIM + slot : RIM + slot + 1, :] = top_ref[lon : lon + 1, :].astype(
                jnp.float32
            )
        sky_copy(way).start()

    cells[2].wait()

    def emit_inside(n, _):
        emit(n + 2 * RIM)
        return 0

    lax.fori_loop(0, lons - 4 * RIM, emit_inside, 0)
    waves[0][FORWARD](0)

    for k, copy in enumerate(piece_copies, 1):
        copy.wait_recv()
        pass_on(k).start()
        if k == chips // 2:
            waves[0][FORWARD](1)
    waves[0][FORWARD](2)

    source = lax.broadcasted_iota(jnp.int32, (2 * lats, 2 * lats), 0) % lats
    target = lax.broadcasted_iota(jnp.int32, (2 * lats, 2 * lats), 1)
    wanted = jnp.where(target < lats, target - 2, target - lats + 2)
    shift_ref[...] = jnp.where(source == wanted, 1.0, 0.0).astype(jnp.bfloat16)

    waves[0][FORWARD](3)
    for k in range(chips):
        pass_on(k).wait_recv()

    piece_count = slot_ref.shape[0]
    for j in range(piece_count):
        held = pieces[slot_ref[j]].astype(jnp.float32)
        rows[j * piece_rows : (j + 1) * piece_rows, :] = held[:piece_rows]
    stack = level_rows * piece_count

    def code_column(lon):
        return rows[pl.ds(lon, stack, stride=pitch), :]

    scales = code_column(lons)

    def wing_copy(way):
        return pltpu.make_async_remote_copy(
            src_ref=wing_out.at[way],
            dst_ref=wing_in.at[way],
            send_sem=wing_sems.at[0, way],
            recv_sem=wing_sems.at[1, way],
            device_id=toward[way],
            device_id_type=MESH,
        )

    for way in (EAST, WEST):
        for slot in (NEAR, FAR):
            lon = last - slot if way == EAST else slot
            wing_out[way, slot * stack : (slot + 1) * stack] = code_column(lon).astype(jnp.bfloat16)
        wing_out[way, 2 * stack : 3 * stack] = scales.astype(jnp.bfloat16)
        third = code_column(last - 2)[0:levels, :]
        wing_out[way, 3 * stack :] = third.astype(jnp.bfloat16)
        wing_copy(way).start()

    for lon in range(lons):
        met[in_met(lon)] = code_column(lon) * scales[:, lon : lon + 1]

    lane = lax.broadcasted_iota(jnp.int32, (levels, lats), 1)
    level = lax.broadcasted_iota(jnp.int32, (levels, lats), 0)

    def east_parts(lon):
        at = in_q1(lon)
        la, lb, lc, ld = face_parts(met[in_met(lon - 1), 0:levels, :])
        ra, rb, rc, rd = face_parts(met[in_met(lon), 0:levels, :])
        coef[at, 0] = la
        coef[at, 1] = lb - ra
        coef[at, 2] = 1.0 + lc - rb
        coef[at, 3] = ld - rc
        coef[at, 4] = -rd

    def other_parts(lon, strength, top):
        at = in_q1(lon)
        column = met[in_met(lon)]
        south = jnp.where(lane > 0, column[levels : 2 * levels, :], 0.0)
        sa, sb, sc, sd = face_parts(south)
        ua, ub, uc, ud = (pltpu.roll(p, lats - 1, 1) for p in (sa, sb, sc, sd))
        air = 1.0 + 0.5 * column[2 * levels : 3 * levels, :]
        cloud = (level < top).astype(jnp.float32)
        weighted = cloud * air
        mass = jnp.sum(weighted, axis=0, keepdims=True)
        keep = 1.0 - strength * cloud
        coef[at, 5] = keep * jnp.where(lane > 1, sa, 0.0)
        coef[at, 6] = keep * jnp.where(lane > 0, sb - ua, 0.0)
        coef[at, 7] = keep * (1.0 + sc - ub)
        coef[at, 8] = keep * jnp.where(lane < lats - 1, sd - uc, 0.0)
        coef[at, 9] = keep * jnp.where(lane < lats - 2, -ud, 0.0)
        coef[at, 10] = strength * weighted / (mass * keep)
        coef[at, 11] = cloud

    def own_other_parts(lon):
        other_parts(lon, strength_ref[pl.ds(lon, 1), :], top_ref[pl.ds(lon, 1), :])

    def inside_parts(lon):
        east_parts(lon)
        own_other_parts(lon)

    group = (lons - 2) // 2

    def some_parts(n, _):
        for u in range(group):
            inside_parts(1 + n * group + u)
        return 0

    waves[1][FORWARD](0)
    lax.fori_loop(0, 2, some_parts, 0)
    inside_parts(last)
    own_other_parts(0)
    waves[1][FORWARD](1)

    def rim_parts(lon):
        way = EAST if lon < 0 else WEST
        slot = -1 - lon if lon < 0 else lon - lons
        east_parts(lon)
        other_parts(
            lon,
            sky_in[way, slot : slot + 1, :],
            sky_in[way, RIM + slot : RIM + slot + 1, :].astype(jnp.int32),
        )

    shift = shift_ref[...]

    def advance(substep, lon, part):
        parts = tuple(coef[in_q1(lon), f] for f in range(FIELDS))
        if substep == 0:
            around = [q0[part, in_q0(lon + d)] for d in (-2, -1, 0, 1, 2)]
            q1[part, in_q1(lon)] = column_step(around, parts, shift)
        else:
            around = [q1[part, in_q1(lon + d)] for d in (-2, -1, 0, 1, 2)]
            out_ref[part, lon] = column_step(around, parts, shift)

    def inside(substep, start, stop):
        def some(n, _):
            for u in range(PAIR):
                advance(substep, start + n * PAIR + u, slice(None))
            return 0

        lax.fori_loop(0, (stop - start) // PAIR, some, 0)

    border = (0, 1, last - 1, last)

    def first_border(blk):
        waves[0][RECEIVE](blk)
        for lon in border:
            advance(0, lon, pl.ds(blk * block, block))

    inside(0, 2, 6)
    waves[1][FORWARD](2)
    inside(0, 6, 10)
    waves[1][FORWARD](3)
    inside(0, 10, lons - 2)

    for way in (EAST, WEST):
        wing_copy(way).wait_recv()
        sky_copy(way).wait_recv()
        near_scales = wing_in[way, 2 * stack : 3 * stack].astype(jnp.float32)
        for slot in (NEAR, FAR):
            theirs = last - slot if way == EAST else slot
            lon = -1 - slot if way == EAST else lons + slot
            code = wing_in[way, slot * stack : (slot + 1) * stack].astype(jnp.float32)
            met[in_met(lon)] = code * near_scales[:, theirs : theirs + 1]
        if way == EAST:
            third = wing_in[way, 3 * stack :].astype(jnp.float32)
            met[0, 0:levels, :] = third * near_scales[0:levels, last - 2 : last - 1]
    east_parts(0)
    for lon in (-2, -1, lons, lons + 1):
        rim_parts(lon)

    each_block(first_border)
    inside(1, 2, lons - 2)

    def finish(blk):
        part = pl.ds(blk * block, block)
        waves[1][RECEIVE](blk)
        for lon in (-2, -1, lons, lons + 1):
            advance(0, lon, part)
        for lon in border:
            advance(1, lon, part)

    each_block(finish)
    each_block(waves[0][DRAIN])
    each_block(waves[1][DRAIN])
    for way in (EAST, WEST):
        sky_copy(way).wait_send()
        wing_copy(way).wait_send()
    for copy in piece_copies:
        copy.wait_send()
    for k in range(chips):
        pass_on(k).wait_send()


def local(tracer_devices, space_devices, tracers, met_codes, met_scales, owner_slot, conv_weight,
          cloud_top, emission, region_tag):
    by_lon = jnp.transpose(tracers, (0, 2, 1, 3))
    count, lons, levels, lats = by_lon.shape
    pieces = owner_slot.shape[0]
    stack = pieces * met_codes.shape[1]
    chips = tracer_devices // CORES
    halo = (count, 2, levels, lats)
    wing = 3 * stack + levels
    piece_rows = met_codes.shape[1] * (lons + 1)
    sent_rows = pl.cdiv(piece_rows, ROW_GROUP) * ROW_GROUP
    hbm = pl.BlockSpec(memory_space=pltpu.HBM)
    dma = pltpu.SemaphoreType.DMA
    out = pl.pallas_call(
        functools.partial(step_kernel, tracer_devices, space_devices),
        out_shape=jax.ShapeDtypeStruct(by_lon.shape, jnp.float32),
        in_specs=[hbm] * 8,
        out_specs=pl.BlockSpec(memory_space=pltpu.VMEM),
        scratch_shapes=[
            pltpu.VMEM((count, lons + 4 * RIM, levels, lats), jnp.float32),
            pltpu.VMEM((count, lons + 2 * RIM, levels, lats), jnp.float32),
            pltpu.VMEM(met_codes.shape, jnp.bfloat16),
            pltpu.VMEM(met_scales.shape, jnp.bfloat16),
            pltpu.SMEM(owner_slot.shape, jnp.int32),
            pltpu.VMEM(conv_weight.shape, jnp.float32),
            pltpu.VMEM(cloud_top.shape, jnp.int32),
            pltpu.VMEM(emission.shape, jnp.float32),
            pltpu.VMEM(region_tag.shape, jnp.int32),
            pltpu.VMEM((pieces, sent_rows, lats), jnp.bfloat16),
            pltpu.VMEM((sent_rows, lats), jnp.float32),
            pltpu.VMEM((pieces * piece_rows, lats), jnp.float32),
            pltpu.VMEM((lons + 2 * RIM + 1, stack, lats), jnp.float32),
            pltpu.VMEM((lons + 2 * RIM, FIELDS, levels, lats), jnp.float32),
            pltpu.VMEM((2 * lats, 2 * lats), jnp.bfloat16),
            pltpu.VMEM((2, 8, lats), jnp.float32),
            pltpu.VMEM((2, 8, lats), jnp.float32),
            pltpu.VMEM((2, wing, lats), jnp.bfloat16),
            pltpu.VMEM((2, wing, lats), jnp.bfloat16),
            pltpu.VMEM((2, 2) + halo, jnp.int16),
            pltpu.VMEM((2, 2) + halo, jnp.int16),
            pltpu.VMEM((2,) + halo, jnp.int16),
            dma((10,)),
            dma((chips,)),
            dma((chips,)),
            dma((chips,)),
            dma((chips,)),
            dma((2, 2)),
            dma((2, 2)),
            dma((2, 2, 2, BLOCKS, 2)),
            dma((2, 2, BLOCKS)),
        ],
        compiler_params=pltpu.CompilerParams(
            collective_id=0, has_side_effects=True, vmem_limit_bytes=48 * 1024 * 1024
        ),
        name="transport_step",
    )(
        *(
            pltpu.with_memory_space_constraint(x, pltpu.HBM)
            for x in (by_lon, met_codes, met_scales, owner_slot, conv_weight, cloud_top, emission)
            + (region_tag,)
        )
    )
    return jnp.transpose(out, (0, 2, 1, 3))


def solution(mesh):
    placed = (
        P("tracer", None, "space", None),
        P("tracer", None, "space", None),
        P("tracer", None, "space"),
        P(),
        P("space", None),
        P("space", None),
        P("space", None),
        P("space", None),
    )
    return jax.shard_map(
        functools.partial(local, mesh.shape["tracer"], mesh.shape["space"]),
        mesh=mesh,
        in_specs=placed,
        out_specs=P("tracer", None, "space", None),
        check_vma=False,
    )
```

```python
import functools

import jax
import jax.numpy as jnp
from jax import lax
from jax.experimental import pallas as pl
from jax.experimental.pallas import tpu as pltpu
from jax.sharding import PartitionSpec as P

MESH = pl.DeviceIdType.MESH
EAST, WEST = 0, 1
NEAR, FAR = 0, 1
RIM = 2
BLOCKS = 4
DIRECT = (3, 2)
STEPS = 1200.0
FLOOR = 24.0
ROW = 4
FIELDS = 12
ROW_GROUP = 16
CORES = 2
PAIR = 2


def face_parts(c):
    size = jnp.abs(c)
    bend = 0.25 * size * (1.0 - size)
    up = c > 0
    zero = jnp.zeros_like(c)
    return (
        jnp.where(up, -bend, zero),
        jnp.where(up, c, -bend),
        jnp.where(up, bend, c),
        jnp.where(up, zero, bend),
    )


def encoded(value):
    size = jnp.maximum(jnp.abs(value), 2.0**-FLOOR)
    steps = jnp.log2(size) * STEPS + (FLOOR * STEPS + 0.5)
    steps = jnp.where(value < 0, -steps, steps)
    return steps.astype(jnp.int32).astype(jnp.int16)


def decoded(code):
    steps = code.astype(jnp.int32).astype(jnp.float32)
    size = jnp.exp2(jnp.abs(steps) * (1.0 / STEPS) - FLOOR)
    return jnp.where(steps < 0, -size, size)


def column_step(cells, parts, shift):
    ea, eb, ec, ed, ee, na, nb, nc, nd, ne, share, cloud = parts
    x = ea * cells[0] + eb * cells[1] + ec * cells[2] + ed * cells[3] + ee * cells[4]
    count, levels, lats = x.shape
    high = x.astype(jnp.bfloat16)
    low = (x - high.astype(jnp.float32)).astype(jnp.bfloat16)
    both = jnp.concatenate([high, low], axis=-1).reshape(count * levels, 2 * lats)
    moved = jnp.dot(both, shift, preferred_element_type=jnp.float32)
    moved = moved.reshape(count, levels, 2 * lats)
    y = (
        nc * x
        + nb * pltpu.roll(x, 1, 2)
        + nd * pltpu.roll(x, lats - 1, 2)
        + na * moved[..., :lats]
        + ne * moved[..., lats:]
    )
    mean = jnp.sum(share * y, axis=-2, keepdims=True)
    return y + cloud * mean


def step_kernel(
    tracer_devices,
    space_devices,
    x_hbm,
    codes_hbm,
    scales_hbm,
    slot_hbm,
    strength_hbm,
    top_hbm,
    emission_hbm,
    tag_hbm,
    out_ref,
    q0,
    q1,
    codes_ref,
    scales_ref,
    slot_ref,
    strength_ref,
    top_ref,
    emission_ref,
    tag_ref,
    pieces,
    staged,
    rows,
    met,
    coef,
    shift_ref,
    sky_out,
    sky_in,
    wing_out,
    wing_in,
    wave_out,
    wave_in,
    wave_relay,
    load_sem,
    piece_send,
    piece_recv,
    pass_send,
    pass_recv,
    sky_sems,
    wing_sems,
    wave_sems,
    relay_sems,
):
    count, lons, levels, lats = x_hbm.shape
    last = lons - 1
    t_me = lax.axis_index("tracer")
    s_me = lax.axis_index("space")
    east = {"space": lax.rem(s_me + 1, space_devices)}
    west = {"space": lax.rem(s_me + space_devices - 1, space_devices)}
    toward = (east, west)
    place = lax.rem(s_me, ROW)
    ends = (place == ROW - 1, place == 0)
    edge = jnp.logical_or(ends[EAST], ends[WEST])

    def along(step):
        return {"space": lax.rem(s_me + step + space_devices, space_devices)}

    hop = (along(1 - ROW), along(ROW - 1))
    relay_way = jnp.where(ends[WEST], EAST, WEST)
    onward = along(jnp.where(ends[WEST], ROW, -ROW))
    sibling = {"tracer": t_me + 1 - 2 * lax.rem(t_me, CORES)}
    chips = tracer_devices // CORES
    block = count // BLOCKS
    level_rows = codes_hbm.shape[1]
    pitch = lons + 1
    piece_rows = level_rows * pitch

    def in_q0(lon):
        return lon + 2 * RIM

    def in_q1(lon):
        return lon + RIM

    def in_met(lon):
        return lon + RIM + 1

    def peer(k):
        return lax.rem(t_me + CORES * k, tracer_devices)

    small = (
        (codes_hbm, codes_ref),
        (scales_hbm, scales_ref),
        (tag_hbm, tag_ref),
        (emission_hbm, emission_ref),
        (slot_hbm, slot_ref),
        (strength_hbm, strength_ref),
        (top_hbm, top_ref),
    )
    loads = [
        pltpu.make_async_copy(src, dst, load_sem.at[n]) for n, (src, dst) in enumerate(small)
    ]
    rims = ((0, 2 * RIM), (lons - 2 * RIM, lons), (2 * RIM, lons - 2 * RIM))
    cells = [
        pltpu.make_async_copy(
            x_hbm.at[:, lo:hi], q0.at[:, in_q0(lo) : in_q0(hi)], load_sem.at[len(small) + n]
        )
        for n, (lo, hi) in enumerate(rims)
    ]
    for copy in loads + cells[:2]:
        copy.start()

    barrier = pltpu.get_barrier_semaphore()
    for k in range(1, chips):
        pl.semaphore_signal(barrier, inc=1, device_id={"tracer": peer(k)}, device_id_type=MESH)
    for to in (sibling, east, west):
        pl.semaphore_signal(barrier, inc=1, device_id=to, device_id_type=MESH)

    @pl.when(edge)
    def _():
        other = along(jnp.where(ends[WEST], ROW - 1, 1 - ROW))
        for to in (other, along(ROW), along(-ROW)):
            pl.semaphore_signal(barrier, inc=1, device_id=to, device_id_type=MESH)

    staged[...] = jnp.zeros_like(staged)
    loads[0].wait()
    loads[1].wait()
    for r in range(level_rows):
        at = r * pitch
        staged[at : at + lons, :] = codes_ref[0, r].astype(jnp.float32)
        staged[at + lons : at + lons + 1, 0:lons] = scales_ref[0, r : r + 1, :].astype(jnp.float32)
    pieces[t_me] = staged[...].astype(jnp.bfloat16)

    pl.semaphore_wait(barrier, chips - 1 + 3 + jnp.where(edge, 3, 0))

    def pass_on(k):
        held = pieces.at[peer(chips - k)]
        return pltpu.make_async_remote_copy(
            src_ref=held,
            dst_ref=held,
            send_sem=pass_send.at[k],
            recv_sem=pass_recv.at[k],
            device_id=sibling,
            device_id_type=MESH,
        )

    piece_copies = []
    for k in range(1, chips):
        copy = pltpu.make_async_remote_copy(
            src_ref=pieces.at[t_me],
            dst_ref=pieces.at[t_me],
            send_sem=piece_send.at[k],
            recv_sem=piece_recv.at[k],
            device_id={"tracer": peer(k)},
            device_id_type=MESH,
        )
        copy.start()
        piece_copies.append(copy)
    pass_on(0).start()

    for copy in loads[2:]:
        copy.wait()
    ids = t_me * count + lax.broadcasted_iota(jnp.int32, (count, 8, lats), 0)
    level_row = lax.broadcasted_iota(jnp.int32, (8, lats), 0)

    def emit(lon):
        tag = jnp.where(level_row == 0, tag_ref[pl.ds(lon, 1), :], -1)
        amount = jnp.broadcast_to(emission_ref[pl.ds(lon, 1), :], (8, lats))
        q0[:, in_q0(lon), 0:8, :] += jnp.where(tag[None] == ids, amount[None], 0.0)

    def each_block(act):
        def one(blk, _):
            act(blk)
            return 0

        lax.fori_loop(0, BLOCKS, one, 0)

    def wave(n):
        out, into, relay = wave_out.at[n], wave_in.at[n], wave_relay.at[n]

        def halves(blk):
            start = blk * block
            return pl.ds(start, DIRECT[n]), pl.ds(start + DIRECT[n], block - DIRECT[n])

        def straight(way, blk, h):
            part = halves(blk)[h]
            return pltpu.make_async_remote_copy(
                src_ref=out.at[way, part],
                dst_ref=into.at[way, part],
                send_sem=wave_sems.at[n, 0, way, blk, h],
                recv_sem=wave_sems.at[n, 1, way, blk, h],
                device_id=toward[way],
                device_id_type=MESH,
            )

        def detour(way, blk):
            part = halves(blk)[1]
            return pltpu.make_async_remote_copy(
                src_ref=out.at[way, part],
                dst_ref=relay.at[part],
                send_sem=wave_sems.at[n, 0, way, blk, 1],
                recv_sem=relay_sems.at[n, 1, blk],
                device_id=hop[way],
                device_id_type=MESH,
            )

        def second_leg(blk):
            part = halves(blk)[1]
            return pltpu.make_async_remote_copy(
                src_ref=relay.at[part],
                dst_ref=into.at[relay_way, part],
                send_sem=relay_sems.at[n, 0, blk],
                recv_sem=wave_sems.at[n, 1, relay_way, blk, 1],
                device_id=onward,
                device_id_type=MESH,
            )

        def send(blk):
            part = pl.ds(blk * block, block)
            for way in (EAST, WEST):
                for slot in (NEAR, FAR):
                    depth = 2 * n + slot
                    lon = last - depth if way == EAST else depth
                    out[way, part, slot] = encoded(q0[part, in_q0(lon)])
            for way in (EAST, WEST):

                @pl.when(ends[way])
                def _(way=way):
                    detour(way, blk).start()

                @pl.when(jnp.logical_not(ends[way]))
                def _(way=way):
                    straight(way, blk, 1).start()

            for way in (EAST, WEST):
                straight(way, blk, 0).start()

        def forward(blk):
            @pl.when(edge)
            def _():
                detour(EAST, blk).wait_recv()
                second_leg(blk).start()

        def receive(way, blk):
            part = pl.ds(blk * block, block)
            for h in (0, 1):
                piece = halves(blk)[h]
                pltpu.make_async_remote_copy(
                    src_ref=out.at[way, piece],
                    dst_ref=into.at[way, piece],
                    send_sem=wave_sems.at[n, 0, way, blk, h],
                    recv_sem=wave_sems.at[n, 1, way, blk, h],
                    device_id=east,
                    device_id_type=MESH,
                ).wait_recv()
            for slot in (NEAR, FAR):
                depth = 2 * n + slot
                lon = jnp.where(way == EAST, -1 - depth, lons + depth)
                q0[part, in_q0(lon)] = decoded(into[way, part, slot])

        def drain(blk):
            for way in (EAST, WEST):
                for h in (0, 1):
                    straight(way, blk, h).wait_send()

            @pl.when(edge)
            def _():
                second_leg(blk).wait_send()

        return send, forward, receive, drain

    waves = (wave(0), wave(1))
    SEND, FORWARD, RECEIVE, DRAIN = range(4)

    cells[0].wait()
    cells[1].wait()
    cells[2].start()
    for lon in (0, 1, last - 1, last):
        emit(lon)
    each_block(waves[0][SEND])
    def take_pieces(start, stop):
        for k in range(start, stop):
            piece_copies[k - 1].wait_recv()
            pass_on(k).start()

    for lon in (2, 3, last - 3, last - 2):
        emit(lon)
    each_block(waves[1][SEND])
    waves[0][FORWARD](0)
    take_pieces(1, chips // 2)
    waves[0][FORWARD](1)
    take_pieces(chips // 2, chips)

    def sky_copy(way):
        return pltpu.make_async_remote_copy(
            src_ref=sky_out.at[way],
            dst_ref=sky_in.at[way],
            send_sem=sky_sems.at[0, way],
            recv_sem=sky_sems.at[1, way],
            device_id=toward[way],
            device_id_type=MESH,
        )

    sky_out[...] = jnp.zeros_like(sky_out)
    for way in (EAST, WEST):
        for slot in (NEAR, FAR):
            lon = last - slot if way == EAST else slot
            sky_out[way, slot : slot + 1, :] = strength_ref[lon : lon + 1, :]
            sky_out[way, RIM + slot : RIM + slot + 1, :] = top_ref[lon : lon + 1, :].astype(
                jnp.float32
            )
        sky_copy(way).start()

    cells[2].wait()

    def emit_inside(n, _):
        emit(n + 2 * RIM)
        return 0

    lax.fori_loop(0, lons - 4 * RIM, emit_inside, 0)
    waves[0][FORWARD](2)

    source = lax.broadcasted_iota(jnp.int32, (2 * lats, 2 * lats), 0) % lats
    target = lax.broadcasted_iota(jnp.int32, (2 * lats, 2 * lats), 1)
    wanted = jnp.where(target < lats, target - 2, target - lats + 2)
    shift_ref[...] = jnp.where(source == wanted, 1.0, 0.0).astype(jnp.bfloat16)

    waves[0][FORWARD](3)
    for k in range(chips):
        pass_on(k).wait_recv()

    piece_count = slot_ref.shape[0]
    for j in range(piece_count):
        held = pieces[slot_ref[j]].astype(jnp.float32)
        rows[j * piece_rows : (j + 1) * piece_rows, :] = held[:piece_rows]
    stack = level_rows * piece_count

    def code_column(lon):
        return rows[pl.ds(lon, stack, stride=pitch), :]

    scales = code_column(lons)

    def wing_copy(way):
        return pltpu.make_async_remote_copy(
            src_ref=wing_out.at[way],
            dst_ref=wing_in.at[way],
            send_sem=wing_sems.at[0, way],
            recv_sem=wing_sems.at[1, way],
            device_id=toward[way],
            device_id_type=MESH,
        )

    for way in (EAST, WEST):
        for slot in (NEAR, FAR):
            lon = last - slot if way == EAST else slot
            wing_out[way, slot * stack : (slot + 1) * stack] = code_column(lon).astype(jnp.bfloat16)
        wing_out[way, 2 * stack : 3 * stack] = scales.astype(jnp.bfloat16)
        third = code_column(last - 2)[0:levels, :]
        wing_out[way, 3 * stack :] = third.astype(jnp.bfloat16)
        wing_copy(way).start()

    for lon in range(lons):
        met[in_met(lon)] = code_column(lon) * scales[:, lon : lon + 1]

    lane = lax.broadcasted_iota(jnp.int32, (levels, lats), 1)
    level = lax.broadcasted_iota(jnp.int32, (levels, lats), 0)

    def east_parts(lon):
        at = in_q1(lon)
        la, lb, lc, ld = face_parts(met[in_met(lon - 1), 0:levels, :])
        ra, rb, rc, rd = face_parts(met[in_met(lon), 0:levels, :])
        coef[at, 0] = la
        coef[at, 1] = lb - ra
        coef[at, 2] = 1.0 + lc - rb
        coef[at, 3] = ld - rc
        coef[at, 4] = -rd

    def other_parts(lon, strength, top):
        at = in_q1(lon)
        column = met[in_met(lon)]
        south = jnp.where(lane > 0, column[levels : 2 * levels, :], 0.0)
        sa, sb, sc, sd = face_parts(south)
        ua, ub, uc, ud = (pltpu.roll(p, lats - 1, 1) for p in (sa, sb, sc, sd))
        air = 1.0 + 0.5 * column[2 * levels : 3 * levels, :]
        cloud = (level < top).astype(jnp.float32)
        weighted = cloud * air
        mass = jnp.sum(weighted, axis=0, keepdims=True)
        keep = 1.0 - strength * cloud
        coef[at, 5] = keep * jnp.where(lane > 1, sa, 0.0)
        coef[at, 6] = keep * jnp.where(lane > 0, sb - ua, 0.0)
        coef[at, 7] = keep * (1.0 + sc - ub)
        coef[at, 8] = keep * jnp.where(lane < lats - 1, sd - uc, 0.0)
        coef[at, 9] = keep * jnp.where(lane < lats - 2, -ud, 0.0)
        coef[at, 10] = strength * weighted / (mass * keep)
        coef[at, 11] = cloud

    def own_other_parts(lon):
        other_parts(lon, strength_ref[pl.ds(lon, 1), :], top_ref[pl.ds(lon, 1), :])

    def inside_parts(lon):
        east_parts(lon)
        own_other_parts(lon)

    group = (lons - 2) // 2

    def some_parts(n, _):
        for u in range(group):
            inside_parts(1 + n * group + u)
        return 0

    waves[1][FORWARD](0)
    waves[1][FORWARD](1)
    lax.fori_loop(0, 2, some_parts, 0)
    inside_parts(last)
    own_other_parts(0)
    waves[1][FORWARD](2)
    waves[1][FORWARD](3)

    def rim_parts(lon):
        way = EAST if lon < 0 else WEST
        slot = -1 - lon if lon < 0 else lon - lons
        east_parts(lon)
        other_parts(
            lon,
            sky_in[way, slot : slot + 1, :],
            sky_in[way, RIM + slot : RIM + slot + 1, :].astype(jnp.int32),
        )

    shift = shift_ref[...]

    def advance(substep, lon, part):
        parts = tuple(coef[in_q1(lon), f] for f in range(FIELDS))
        if substep == 0:
            around = [q0[part, in_q0(lon + d)] for d in (-2, -1, 0, 1, 2)]
            q1[part, in_q1(lon)] = column_step(around, parts, shift)
        else:
            around = [q1[part, in_q1(lon + d)] for d in (-2, -1, 0, 1, 2)]
            out_ref[part, lon] = column_step(around, parts, shift)

    def inside(substep, start, stop):
        def some(n, _):
            for u in range(PAIR):
                advance(substep, start + n * PAIR + u, slice(None))
            return 0

        lax.fori_loop(0, (stop - start) // PAIR, some, 0)

    border = (0, 1, last - 1, last)

    def first_border(blk):
        for way in (EAST, WEST):
            waves[0][RECEIVE](way, blk)
        for lon in border:
            advance(0, lon, pl.ds(blk * block, block))

    inside(0, 2, lons - 2)

    for way in (EAST, WEST):
        wing_copy(way).wait_recv()
        sky_copy(way).wait_recv()
        near_scales = wing_in[way, 2 * stack : 3 * stack].astype(jnp.float32)
        for slot in (NEAR, FAR):
            theirs = last - slot if way == EAST else slot
            lon = -1 - slot if way == EAST else lons + slot
            code = wing_in[way, slot * stack : (slot + 1) * stack].astype(jnp.float32)
            met[in_met(lon)] = code * near_scales[:, theirs : theirs + 1]
        if way == EAST:
            third = wing_in[way, 3 * stack :].astype(jnp.float32)
            met[0, 0:levels, :] = third * near_scales[0:levels, last - 2 : last - 1]
    east_parts(0)
    for lon in (-2, -1, lons, lons + 1):
        rim_parts(lon)

    each_block(first_border)
    inside(1, 2, lons - 2)

    def finish(way, start, stop):
        part = pl.ds(start * block, (stop - start) * block)
        for blk in range(start, stop):
            waves[1][RECEIVE](way, blk)
        for depth in (0, 1):
            advance(0, jnp.where(way == EAST, -1 - depth, lons + depth), part)
        for depth in (0, 1):
            advance(1, jnp.where(way == EAST, depth, last - depth), part)

    late = jnp.where(ends[WEST], EAST, WEST)
    finish(1 - late, 0, BLOCKS)
    finish(late, 0, BLOCKS // 2)
    finish(late, BLOCKS // 2, BLOCKS)
    each_block(waves[0][DRAIN])
    each_block(waves[1][DRAIN])
    for way in (EAST, WEST):
        sky_copy(way).wait_send()
        wing_copy(way).wait_send()
    for copy in piece_copies:
        copy.wait_send()
    for k in range(chips):
        pass_on(k).wait_send()


def local(tracer_devices, space_devices, tracers, met_codes, met_scales, owner_slot, conv_weight,
          cloud_top, emission, region_tag):
    by_lon = jnp.transpose(tracers, (0, 2, 1, 3))
    count, lons, levels, lats = by_lon.shape
    pieces = owner_slot.shape[0]
    stack = pieces * met_codes.shape[1]
    chips = tracer_devices // CORES
    halo = (count, 2, levels, lats)
    wing = 3 * stack + levels
    piece_rows = met_codes.shape[1] * (lons + 1)
    sent_rows = pl.cdiv(piece_rows, ROW_GROUP) * ROW_GROUP
    hbm = pl.BlockSpec(memory_space=pltpu.HBM)
    dma = pltpu.SemaphoreType.DMA
    out = pl.pallas_call(
        functools.partial(step_kernel, tracer_devices, space_devices),
        out_shape=jax.ShapeDtypeStruct(by_lon.shape, jnp.float32),
        in_specs=[hbm] * 8,
        out_specs=pl.BlockSpec(memory_space=pltpu.VMEM),
        scratch_shapes=[
            pltpu.VMEM((count, lons + 4 * RIM, levels, lats), jnp.float32),
            pltpu.VMEM((count, lons + 2 * RIM, levels, lats), jnp.float32),
            pltpu.VMEM(met_codes.shape, jnp.bfloat16),
            pltpu.VMEM(met_scales.shape, jnp.bfloat16),
            pltpu.SMEM(owner_slot.shape, jnp.int32),
            pltpu.VMEM(conv_weight.shape, jnp.float32),
            pltpu.VMEM(cloud_top.shape, jnp.int32),
            pltpu.VMEM(emission.shape, jnp.float32),
            pltpu.VMEM(region_tag.shape, jnp.int32),
            pltpu.VMEM((pieces, sent_rows, lats), jnp.bfloat16),
            pltpu.VMEM((sent_rows, lats), jnp.float32),
            pltpu.VMEM((pieces * piece_rows, lats), jnp.float32),
            pltpu.VMEM((lons + 2 * RIM + 1, stack, lats), jnp.float32),
            pltpu.VMEM((lons + 2 * RIM, FIELDS, levels, lats), jnp.float32),
            pltpu.VMEM((2 * lats, 2 * lats), jnp.bfloat16),
            pltpu.VMEM((2, 8, lats), jnp.float32),
            pltpu.VMEM((2, 8, lats), jnp.float32),
            pltpu.VMEM((2, wing, lats), jnp.bfloat16),
            pltpu.VMEM((2, wing, lats), jnp.bfloat16),
            pltpu.VMEM((2, 2) + halo, jnp.int16),
            pltpu.VMEM((2, 2) + halo, jnp.int16),
            pltpu.VMEM((2,) + halo, jnp.int16),
            dma((10,)),
            dma((chips,)),
            dma((chips,)),
            dma((chips,)),
            dma((chips,)),
            dma((2, 2)),
            dma((2, 2)),
            dma((2, 2, 2, BLOCKS, 2)),
            dma((2, 2, BLOCKS)),
        ],
        compiler_params=pltpu.CompilerParams(
            collective_id=0, has_side_effects=True, vmem_limit_bytes=48 * 1024 * 1024
        ),
        name="transport_step",
    )(
        *(
            pltpu.with_memory_space_constraint(x, pltpu.HBM)
            for x in (by_lon, met_codes, met_scales, owner_slot, conv_weight, cloud_top, emission)
            + (region_tag,)
        )
    )
    return jnp.transpose(out, (0, 2, 1, 3))


def solution(mesh):
    placed = (
        P("tracer", None, "space", None),
        P("tracer", None, "space", None),
        P("tracer", None, "space"),
        P(),
        P("space", None),
        P("space", None),
        P("space", None),
        P("space", None),
    )
    return jax.shard_map(
        functools.partial(local, mesh.shape["tracer"], mesh.shape["space"]),
        mesh=mesh,
        in_specs=placed,
        out_specs=P("tracer", None, "space", None),
        check_vma=False,
    )
```

```python
import functools

import jax
import jax.numpy as jnp
from jax import lax
from jax.experimental import pallas as pl
from jax.experimental.pallas import tpu as pltpu
from jax.sharding import PartitionSpec as P

MESH = pl.DeviceIdType.MESH
EAST, WEST = 0, 1
NEAR, FAR = 0, 1
RIM = 2
BLOCKS = 4
DIRECT = (4, 2)
STEPS = 1200.0
FLOOR = 24.0
ROW = 4
FIELDS = 12
ROW_GROUP = 16
CORES = 2
PAIR = 2


def face_parts(c):
    size = jnp.abs(c)
    bend = 0.25 * size * (1.0 - size)
    up = c > 0
    zero = jnp.zeros_like(c)
    return (
        jnp.where(up, -bend, zero),
        jnp.where(up, c, -bend),
        jnp.where(up, bend, c),
        jnp.where(up, zero, bend),
    )


def encoded(value):
    size = jnp.maximum(jnp.abs(value), 2.0**-FLOOR)
    steps = jnp.log2(size) * STEPS + (FLOOR * STEPS + 0.5)
    steps = jnp.where(value < 0, -steps, steps)
    return steps.astype(jnp.int32).astype(jnp.int16)


def decoded(code):
    steps = code.astype(jnp.int32).astype(jnp.float32)
    size = jnp.exp2(jnp.abs(steps) * (1.0 / STEPS) - FLOOR)
    return jnp.where(steps < 0, -size, size)


def column_step(cells, parts, shift):
    ea, eb, ec, ed, ee, na, nb, nc, nd, ne, share, cloud = parts
    x = ea * cells[0] + eb * cells[1] + ec * cells[2] + ed * cells[3] + ee * cells[4]
    count, levels, lats = x.shape
    high = x.astype(jnp.bfloat16)
    low = (x - high.astype(jnp.float32)).astype(jnp.bfloat16)
    both = jnp.concatenate([high, low], axis=-1).reshape(count * levels, 2 * lats)
    moved = jnp.dot(both, shift, preferred_element_type=jnp.float32)
    moved = moved.reshape(count, levels, 2 * lats)
    y = (
        nc * x
        + nb * pltpu.roll(x, 1, 2)
        + nd * pltpu.roll(x, lats - 1, 2)
        + na * moved[..., :lats]
        + ne * moved[..., lats:]
    )
    mean = jnp.sum(share * y, axis=-2, keepdims=True)
    return y + cloud * mean


def step_kernel(
    tracer_devices,
    space_devices,
    x_hbm,
    codes_hbm,
    scales_hbm,
    slot_hbm,
    strength_hbm,
    top_hbm,
    emission_hbm,
    tag_hbm,
    out_ref,
    q0,
    q1,
    codes_ref,
    scales_ref,
    slot_ref,
    strength_ref,
    top_ref,
    emission_ref,
    tag_ref,
    pieces,
    staged,
    rows,
    met,
    coef,
    shift_ref,
    sky_out,
    sky_in,
    wing_out,
    wing_in,
    wave_out,
    wave_in,
    wave_relay,
    load_sem,
    piece_send,
    piece_recv,
    pass_send,
    pass_recv,
    sky_sems,
    wing_sems,
    wave_sems,
    relay_sems,
):
    count, lons, levels, lats = x_hbm.shape
    last = lons - 1
    t_me = lax.axis_index("tracer")
    s_me = lax.axis_index("space")
    east = {"space": lax.rem(s_me + 1, space_devices)}
    west = {"space": lax.rem(s_me + space_devices - 1, space_devices)}
    toward = (east, west)
    place = lax.rem(s_me, ROW)
    ends = (place == ROW - 1, place == 0)
    edge = jnp.logical_or(ends[EAST], ends[WEST])

    def along(step):
        return {"space": lax.rem(s_me + step + space_devices, space_devices)}

    hop = (along(1 - ROW), along(ROW - 1))
    relay_way = jnp.where(ends[WEST], EAST, WEST)
    onward = along(jnp.where(ends[WEST], ROW, -ROW))
    sibling = {"tracer": t_me + 1 - 2 * lax.rem(t_me, CORES)}
    chips = tracer_devices // CORES
    block = count // BLOCKS
    level_rows = codes_hbm.shape[1]
    pitch = lons + 1
    piece_rows = level_rows * pitch

    def in_q0(lon):
        return lon + 2 * RIM

    def in_q1(lon):
        return lon + RIM

    def in_met(lon):
        return lon + RIM + 1

    def peer(k):
        return lax.rem(t_me + CORES * k, tracer_devices)

    small = (
        (codes_hbm, codes_ref),
        (scales_hbm, scales_ref),
        (tag_hbm, tag_ref),
        (emission_hbm, emission_ref),
        (slot_hbm, slot_ref),
        (strength_hbm, strength_ref),
        (top_hbm, top_ref),
    )
    loads = [
        pltpu.make_async_copy(src, dst, load_sem.at[n]) for n, (src, dst) in enumerate(small)
    ]
    cuts = (0, RIM, 2 * RIM, lons - 2 * RIM, lons - RIM, lons)
    rims = [cuts[n : n + 2] for n in (0, 4, 1, 3, 2)]
    cells = [
        pltpu.make_async_copy(
            x_hbm.at[:, lo:hi], q0.at[:, in_q0(lo) : in_q0(hi)], load_sem.at[len(small) + n]
        )
        for n, (lo, hi) in enumerate(rims)
    ]
    for copy in loads + cells[:4]:
        copy.start()

    barrier = pltpu.get_barrier_semaphore()
    for k in range(1, chips):
        pl.semaphore_signal(barrier, inc=1, device_id={"tracer": peer(k)}, device_id_type=MESH)
    for to in (sibling, east, west):
        pl.semaphore_signal(barrier, inc=1, device_id=to, device_id_type=MESH)

    @pl.when(edge)
    def _():
        other = along(jnp.where(ends[WEST], ROW - 1, 1 - ROW))
        for to in (other, along(ROW), along(-ROW)):
            pl.semaphore_signal(barrier, inc=1, device_id=to, device_id_type=MESH)

    staged[...] = jnp.zeros_like(staged)
    loads[0].wait()
    loads[1].wait()
    for r in range(level_rows):
        at = r * pitch
        staged[at : at + lons, :] = codes_ref[0, r].astype(jnp.float32)
        staged[at + lons : at + lons + 1, 0:lons] = scales_ref[0, r : r + 1, :].astype(jnp.float32)
    pieces[t_me] = staged[...].astype(jnp.bfloat16)

    pl.semaphore_wait(barrier, chips - 1 + 3 + jnp.where(edge, 3, 0))

    def pass_on(k):
        held = pieces.at[peer(chips - k)]
        return pltpu.make_async_remote_copy(
            src_ref=held,
            dst_ref=held,
            send_sem=pass_send.at[k],
            recv_sem=pass_recv.at[k],
            device_id=sibling,
            device_id_type=MESH,
        )

    piece_copies = []
    for k in range(1, chips):
        copy = pltpu.make_async_remote_copy(
            src_ref=pieces.at[t_me],
            dst_ref=pieces.at[t_me],
            send_sem=piece_send.at[k],
            recv_sem=piece_recv.at[k],
            device_id={"tracer": peer(k)},
            device_id_type=MESH,
        )
        copy.start()
        piece_copies.append(copy)
    pass_on(0).start()

    for copy in loads[2:]:
        copy.wait()
    ids = t_me * count + lax.broadcasted_iota(jnp.int32, (count, 8, lats), 0)
    level_row = lax.broadcasted_iota(jnp.int32, (8, lats), 0)

    def emit(lon):
        tag = jnp.where(level_row == 0, tag_ref[pl.ds(lon, 1), :], -1)
        amount = jnp.broadcast_to(emission_ref[pl.ds(lon, 1), :], (8, lats))
        q0[:, in_q0(lon), 0:8, :] += jnp.where(tag[None] == ids, amount[None], 0.0)

    def each_block(act):
        def one(blk, _):
            act(blk)
            return 0

        lax.fori_loop(0, BLOCKS, one, 0)

    def wave(n):
        out, into, relay = wave_out.at[n], wave_in.at[n], wave_relay.at[n]

        def halves(blk):
            start = blk * block
            return pl.ds(start, DIRECT[n]), pl.ds(start + DIRECT[n], block - DIRECT[n])

        def straight(way, blk, h):
            part = halves(blk)[h]
            return pltpu.make_async_remote_copy(
                src_ref=out.at[way, part],
                dst_ref=into.at[way, part],
                send_sem=wave_sems.at[n, 0, way, blk, h],
                recv_sem=wave_sems.at[n, 1, way, blk, h],
                device_id=toward[way],
                device_id_type=MESH,
            )

        def detour(way, blk):
            part = halves(blk)[1]
            return pltpu.make_async_remote_copy(
                src_ref=out.at[way, part],
                dst_ref=relay.at[part],
                send_sem=wave_sems.at[n, 0, way, blk, 1],
                recv_sem=relay_sems.at[n, 1, blk],
                device_id=hop[way],
                device_id_type=MESH,
            )

        def second_leg(blk):
            part = halves(blk)[1]
            return pltpu.make_async_remote_copy(
                src_ref=relay.at[part],
                dst_ref=into.at[relay_way, part],
                send_sem=relay_sems.at[n, 0, blk],
                recv_sem=wave_sems.at[n, 1, relay_way, blk, 1],
                device_id=onward,
                device_id_type=MESH,
            )

        def send(blk):
            part = pl.ds(blk * block, block)
            for way in (EAST, WEST):
                for slot in (NEAR, FAR):
                    depth = 2 * n + slot
                    lon = last - depth if way == EAST else depth
                    out[way, part, slot] = encoded(q0[part, in_q0(lon)])
            for way in (EAST, WEST):

                @pl.when(ends[way])
                def _(way=way):
                    detour(way, blk).start()

                @pl.when(jnp.logical_not(ends[way]))
                def _(way=way):
                    straight(way, blk, 1).start()

            for way in (EAST, WEST):
                straight(way, blk, 0).start()

        def forward(blk):
            @pl.when(edge)
            def _():
                detour(EAST, blk).wait_recv()
                second_leg(blk).start()

        def receive(way, blk):
            part = pl.ds(blk * block, block)
            for h in (0, 1):
                piece = halves(blk)[h]
                pltpu.make_async_remote_copy(
                    src_ref=out.at[way, piece],
                    dst_ref=into.at[way, piece],
                    send_sem=wave_sems.at[n, 0, way, blk, h],
                    recv_sem=wave_sems.at[n, 1, way, blk, h],
                    device_id=east,
                    device_id_type=MESH,
                ).wait_recv()
            for slot in (NEAR, FAR):
                depth = 2 * n + slot
                lon = jnp.where(way == EAST, -1 - depth, lons + depth)
                q0[part, in_q0(lon)] = decoded(into[way, part, slot])

        def drain(blk):
            for way in (EAST, WEST):
                for h in (0, 1):
                    straight(way, blk, h).wait_send()

            @pl.when(edge)
            def _():
                second_leg(blk).wait_send()

        return send, forward, receive, drain

    waves = (wave(0), wave(1))
    SEND, FORWARD, RECEIVE, DRAIN = range(4)

    cells[0].wait()
    cells[1].wait()
    cells[4].start()
    for lon in (0, 1, last - 1, last):
        emit(lon)
    each_block(waves[0][SEND])
    def take_pieces(start, stop):
        for k in range(start, stop):
            piece_copies[k - 1].wait_recv()
            pass_on(k).start()

    cells[2].wait()
    cells[3].wait()
    for lon in (2, 3, last - 3, last - 2):
        emit(lon)
    each_block(waves[1][SEND])
    waves[0][FORWARD](0)
    take_pieces(1, chips // 2)
    waves[0][FORWARD](1)
    take_pieces(chips // 2, chips)

    def sky_copy(way):
        return pltpu.make_async_remote_copy(
            src_ref=sky_out.at[way],
            dst_ref=sky_in.at[way],
            send_sem=sky_sems.at[0, way],
            recv_sem=sky_sems.at[1, way],
            device_id=toward[way],
            device_id_type=MESH,
        )

    sky_out[...] = jnp.zeros_like(sky_out)
    for way in (EAST, WEST):
        for slot in (NEAR, FAR):
            lon = last - slot if way == EAST else slot
            sky_out[way, slot : slot + 1, :] = strength_ref[lon : lon + 1, :]
            sky_out[way, RIM + slot : RIM + slot + 1, :] = top_ref[lon : lon + 1, :].astype(
                jnp.float32
            )
        sky_copy(way).start()

    cells[4].wait()

    def emit_inside(n, _):
        emit(n + 2 * RIM)
        return 0

    lax.fori_loop(0, lons - 4 * RIM, emit_inside, 0)
    waves[0][FORWARD](2)

    source = lax.broadcasted_iota(jnp.int32, (2 * lats, 2 * lats), 0) % lats
    target = lax.broadcasted_iota(jnp.int32, (2 * lats, 2 * lats), 1)
    wanted = jnp.where(target < lats, target - 2, target - lats + 2)
    shift_ref[...] = jnp.where(source == wanted, 1.0, 0.0).astype(jnp.bfloat16)

    waves[0][FORWARD](3)
    for k in range(chips):
        pass_on(k).wait_recv()

    piece_count = slot_ref.shape[0]
    for j in range(piece_count):
        held = pieces[slot_ref[j]].astype(jnp.float32)
        rows[j * piece_rows : (j + 1) * piece_rows, :] = held[:piece_rows]
    stack = level_rows * piece_count

    def code_column(lon):
        return rows[pl.ds(lon, stack, stride=pitch), :]

    scales = code_column(lons)

    def wing_copy(way):
        part = pl.ds(0, 3 * stack + (levels if way == EAST else 0))
        return pltpu.make_async_remote_copy(
            src_ref=wing_out.at[way, part],
            dst_ref=wing_in.at[way, part],
            send_sem=wing_sems.at[0, way],
            recv_sem=wing_sems.at[1, way],
            device_id=toward[way],
            device_id_type=MESH,
        )

    for way in (EAST, WEST):
        for slot in (NEAR, FAR):
            lon = last - slot if way == EAST else slot
            wing_out[way, slot * stack : (slot + 1) * stack] = code_column(lon).astype(jnp.bfloat16)
        wing_out[way, 2 * stack : 3 * stack] = scales.astype(jnp.bfloat16)
        if way == EAST:
            third = code_column(last - 2)[0:levels, :]
            wing_out[way, 3 * stack :] = third.astype(jnp.bfloat16)
        wing_copy(way).start()

    for lon in range(lons):
        met[in_met(lon)] = code_column(lon) * scales[:, lon : lon + 1]

    lane = lax.broadcasted_iota(jnp.int32, (levels, lats), 1)
    level = lax.broadcasted_iota(jnp.int32, (levels, lats), 0)

    def face(lon):
        return face_parts(met[in_met(lon), 0:levels, :])

    def east_parts(lon, left=None):
        at = in_q1(lon)
        la, lb, lc, ld = face(lon - 1) if left is None else left
        ra, rb, rc, rd = right = face(lon)
        coef[at, 0] = la
        coef[at, 1] = lb - ra
        coef[at, 2] = 1.0 + lc - rb
        coef[at, 3] = ld - rc
        coef[at, 4] = -rd
        return right

    def other_parts(lon, strength, top):
        at = in_q1(lon)
        column = met[in_met(lon)]
        south = jnp.where(lane > 0, column[levels : 2 * levels, :], 0.0)
        sa, sb, sc, sd = face_parts(south)
        ua, ub, uc, ud = (pltpu.roll(p, lats - 1, 1) for p in (sa, sb, sc, sd))
        air = 1.0 + 0.5 * column[2 * levels : 3 * levels, :]
        cloud = (level < top).astype(jnp.float32)
        weighted = cloud * air
        mass = jnp.sum(weighted, axis=0, keepdims=True)
        keep = 1.0 - strength * cloud
        coef[at, 5] = keep * jnp.where(lane > 1, sa, 0.0)
        coef[at, 6] = keep * jnp.where(lane > 0, sb - ua, 0.0)
        coef[at, 7] = keep * (1.0 + sc - ub)
        coef[at, 8] = keep * jnp.where(lane < lats - 1, sd - uc, 0.0)
        coef[at, 9] = keep * jnp.where(lane < lats - 2, -ud, 0.0)
        coef[at, 10] = strength * weighted / (mass * keep)
        coef[at, 11] = cloud

    def own_other_parts(lon):
        other_parts(lon, strength_ref[pl.ds(lon, 1), :], top_ref[pl.ds(lon, 1), :])

    def inside_parts(lon, left=None):
        right = east_parts(lon, left)
        own_other_parts(lon)
        return right

    group = (lons - 2) // 2

    def some_parts(n, _):
        left = None
        for u in range(group):
            left = inside_parts(1 + n * group + u, left)
        return 0

    waves[1][FORWARD](0)
    waves[1][FORWARD](1)
    lax.fori_loop(0, 2, some_parts, 0)
    inside_parts(last)
    own_other_parts(0)
    waves[1][FORWARD](2)
    waves[1][FORWARD](3)

    def rim_parts(lon):
        way = EAST if lon < 0 else WEST
        slot = -1 - lon if lon < 0 else lon - lons
        east_parts(lon)
        other_parts(
            lon,
            sky_in[way, slot : slot + 1, :],
            sky_in[way, RIM + slot : RIM + slot + 1, :].astype(jnp.int32),
        )

    shift = shift_ref[...]

    def advance(substep, lon, part):
        parts = tuple(coef[in_q1(lon), f] for f in range(FIELDS))
        if substep == 0:
            around = [q0[part, in_q0(lon + d)] for d in (-2, -1, 0, 1, 2)]
            q1[part, in_q1(lon)] = column_step(around, parts, shift)
        else:
            around = [q1[part, in_q1(lon + d)] for d in (-2, -1, 0, 1, 2)]
            out_ref[part, lon] = column_step(around, parts, shift)

    def inside(substep, start, stop):
        def some(n, _):
            for u in range(PAIR):
                advance(substep, start + n * PAIR + u, slice(None))
            return 0

        lax.fori_loop(0, (stop - start) // PAIR, some, 0)

    border = (0, 1, last - 1, last)

    def first_border(half):
        for way in (EAST, WEST):
            for u in (0, 1):
                waves[0][RECEIVE](way, 2 * half + u)
        for lon in border:
            advance(0, lon, pl.ds(half * 2 * block, 2 * block))

    inside(0, 2, lons - 2)

    for way in (EAST, WEST):
        wing_copy(way).wait_recv()
        sky_copy(way).wait_recv()
        near_scales = wing_in[way, 2 * stack : 3 * stack].astype(jnp.float32)
        for slot in (NEAR, FAR):
            theirs = last - slot if way == EAST else slot
            lon = -1 - slot if way == EAST else lons + slot
            code = wing_in[way, slot * stack : (slot + 1) * stack].astype(jnp.float32)
            met[in_met(lon)] = code * near_scales[:, theirs : theirs + 1]
        if way == EAST:
            third = wing_in[way, 3 * stack :].astype(jnp.float32)
            met[0, 0:levels, :] = third * near_scales[0:levels, last - 2 : last - 1]
    east_parts(0)
    for lon in (-2, -1, lons, lons + 1):
        rim_parts(lon)

    for half in range(BLOCKS // 2):
        first_border(half)
    inside(1, 2, lons - 2)

    def finish(way, start, stop):
        part = pl.ds(start * block, (stop - start) * block)
        for blk in range(start, stop):
            waves[1][RECEIVE](way, blk)
        for depth in (0, 1):
            advance(0, jnp.where(way == EAST, -1 - depth, lons + depth), part)
        for depth in (0, 1):
            advance(1, jnp.where(way == EAST, depth, last - depth), part)

    late = jnp.where(ends[WEST], EAST, WEST)
    finish(1 - late, 0, BLOCKS)
    finish(late, 0, BLOCKS // 2)
    finish(late, BLOCKS // 2, BLOCKS)
    each_block(waves[0][DRAIN])
    each_block(waves[1][DRAIN])
    for way in (EAST, WEST):
        sky_copy(way).wait_send()
        wing_copy(way).wait_send()
    for copy in piece_copies:
        copy.wait_send()
    for k in range(chips):
        pass_on(k).wait_send()


def local(tracer_devices, space_devices, tracers, met_codes, met_scales, owner_slot, conv_weight,
          cloud_top, emission, region_tag):
    by_lon = jnp.transpose(tracers, (0, 2, 1, 3))
    count, lons, levels, lats = by_lon.shape
    pieces = owner_slot.shape[0]
    stack = pieces * met_codes.shape[1]
    chips = tracer_devices // CORES
    halo = (count, 2, levels, lats)
    wing = 3 * stack + levels
    piece_rows = met_codes.shape[1] * (lons + 1)
    sent_rows = pl.cdiv(piece_rows, ROW_GROUP) * ROW_GROUP
    hbm = pl.BlockSpec(memory_space=pltpu.HBM)
    dma = pltpu.SemaphoreType.DMA
    out = pl.pallas_call(
        functools.partial(step_kernel, tracer_devices, space_devices),
        out_shape=jax.ShapeDtypeStruct(by_lon.shape, jnp.float32),
        in_specs=[hbm] * 8,
        out_specs=pl.BlockSpec(memory_space=pltpu.VMEM),
        scratch_shapes=[
            pltpu.VMEM((count, lons + 4 * RIM, levels, lats), jnp.float32),
            pltpu.VMEM((count, lons + 2 * RIM, levels, lats), jnp.float32),
            pltpu.VMEM(met_codes.shape, jnp.bfloat16),
            pltpu.VMEM(met_scales.shape, jnp.bfloat16),
            pltpu.SMEM(owner_slot.shape, jnp.int32),
            pltpu.VMEM(conv_weight.shape, jnp.float32),
            pltpu.VMEM(cloud_top.shape, jnp.int32),
            pltpu.VMEM(emission.shape, jnp.float32),
            pltpu.VMEM(region_tag.shape, jnp.int32),
            pltpu.VMEM((pieces, sent_rows, lats), jnp.bfloat16),
            pltpu.VMEM((sent_rows, lats), jnp.float32),
            pltpu.VMEM((pieces * piece_rows, lats), jnp.float32),
            pltpu.VMEM((lons + 2 * RIM + 1, stack, lats), jnp.float32),
            pltpu.VMEM((lons + 2 * RIM, FIELDS, levels, lats), jnp.float32),
            pltpu.VMEM((2 * lats, 2 * lats), jnp.bfloat16),
            pltpu.VMEM((2, 8, lats), jnp.float32),
            pltpu.VMEM((2, 8, lats), jnp.float32),
            pltpu.VMEM((2, wing, lats), jnp.bfloat16),
            pltpu.VMEM((2, wing, lats), jnp.bfloat16),
            pltpu.VMEM((2, 2) + halo, jnp.int16),
            pltpu.VMEM((2, 2) + halo, jnp.int16),
            pltpu.VMEM((2,) + halo, jnp.int16),
            dma((12,)),
            dma((chips,)),
            dma((chips,)),
            dma((chips,)),
            dma((chips,)),
            dma((2, 2)),
            dma((2, 2)),
            dma((2, 2, 2, BLOCKS, 2)),
            dma((2, 2, BLOCKS)),
        ],
        compiler_params=pltpu.CompilerParams(
            collective_id=0, has_side_effects=True, vmem_limit_bytes=48 * 1024 * 1024
        ),
        name="transport_step",
    )(
        *(
            pltpu.with_memory_space_constraint(x, pltpu.HBM)
            for x in (by_lon, met_codes, met_scales, owner_slot, conv_weight, cloud_top, emission)
            + (region_tag,)
        )
    )
    return jnp.transpose(out, (0, 2, 1, 3))


def solution(mesh):
    placed = (
        P("tracer", None, "space", None),
        P("tracer", None, "space", None),
        P("tracer", None, "space"),
        P(),
        P("space", None),
        P("space", None),
        P("space", None),
        P("space", None),
    )
    return jax.shard_map(
        functools.partial(local, mesh.shape["tracer"], mesh.shape["space"]),
        mesh=mesh,
        in_specs=placed,
        out_specs=P("tracer", None, "space", None),
        check_vma=False,
    )
```
